32 devices in a mesh: narrow: 4 (over x, core), wide: 8 (over z, y).
Axes of the slice: x: 2, y: 2, z: 4, core: 2. Of those that a mesh axis runs over, the one named last changes fastest.
Arguments:
- tokens: bfloat16 [8, 1024, 1024], P('wide', 'narrow'), may hold values from -6 to 6
- segments: int32 [8, 1024], P('wide'), may hold values from 0 to 8, as said below
- routes: int32 [8192, 1], P(('narrow', 'wide')), may hold values from 0 to 7; in each aligned block of 256 rows (0 to 255, 256 to 511, ...) at most 64 rows name the same one
- w_qkv: bfloat16 [1024, 3072], replicated, may hold values from -0.1875 to 0.1875
- w_out: bfloat16 [1024, 1024], replicated, may hold values from -1 to 1
- w_fc1: bfloat16 [1024, 4096], replicated, may hold values from -0.1875 to 0.1875
- w_fc2: bfloat16 [4096, 1024], replicated, may hold values from -0.1875 to 0.1875
- router: bfloat16 [1024, 8], replicated, may hold values from -0.09375 to 0.09375
- mix_weight: bfloat16 [1024, 2], replicated, may hold values from -0.1875 to 0.1875
- gain_one: bfloat16 [1024], replicated, may hold values from 0.5 to 1.5
- gain_two: bfloat16 [1024], replicated, may hold values from 0.5 to 1.5
- expert_in: bfloat16 [8, 1024, 4096], P('wide'), may hold values from -0.1875 to 0.1875
- expert_out: bfloat16 [8, 4096, 1024], P('wide'), may hold values from -1 to 1
- cotangent: bfloat16 [8, 1024, 1024], P('wide', 'narrow'), may hold values from -6 to 6
Outputs:
- output: bfloat16 [8, 1024, 1024], P('wide', 'narrow')
- input_grad: float32 [8, 1024, 1024], P('wide', 'narrow')
- grad_qkv: float32 [1024, 3072], P('wide')
- grad_out: float32 [1024, 1024], P('wide')
- grad_fc1: float32 [1024, 4096], P('wide')
- grad_fc2: float32 [4096, 1024], P('wide')
- grad_router: float32 [1024, 8], P('wide')
- grad_mix: float32 [1024, 2], P('wide')
- grad_gain_one: float32 [1024], P('wide')
- grad_gain_two: float32 [1024], P('wide')
- grad_expert_in: float32 [8, 1024, 4096], P('wide', 'narrow')
- grad_expert_out: float32 [8, 4096, 1024], P('wide', 'narrow')
The draws below stay inside these ranges and needn't reach their ends.
Inputs may be any that keep to these rules, and one draw needn't show every extreme that they name: `routes`: in each aligned block of 256 rows (the rows of one device) no expert is named more than 64 times. `segments`: never decreases along a sequence and starts at 0.
All inputs are finite; a program needn't handle non-finite values.
Results may differ from the reference program's by a relative error of at most 0.015.
Values may be sent and summed in bfloat16 or wider, within the bound.
No kernel may reach another device: no remote copies, remote signals or barrier semaphores. Data moves between devices by JAX's collectives and lax.ppermute only.
A program may use at most 256 MiB of HBM per device.

```python
import math
import jax
import jax.numpy as jnp
import numpy as np
from jax import lax

D = 1024
HEADS = 16
HEAD_DIM = 64
FF = 4096
SEQ_W = 1
LEN_DEV = 256
EXPERTS = 8
TOK_DEV = 256
LENGTH = 1024
SEQS = 8
TOKENS = 8192
CAP = 64
N_NARROW = 4
N_WIDE = 8


def draw_segments(key, part):
    key = jax.random.fold_in(key, 5)
    streams = jax.random.split(key, 2)
    position = jnp.arange(LENGTH)[None, :]
    opening = jax.random.randint(streams[0], (SEQS, 1), LEN_DEV // 4, LEN_DEV // 2 + 1)
    finish = jax.random.randint(streams[1], (SEQS, 1), LENGTH - LEN_DEV // 2, LENGTH - LEN_DEV // 4)
    tail_start = finish + 1
    tail_len = LENGTH - tail_start
    marks = [opening, tail_start]
    for quarter in (1, 2, 3):
        marks.append(opening * quarter // 4)
        marks.append(tail_start + tail_len * quarter // 4)
    boundary = jnp.zeros((SEQS, LENGTH), jnp.int32)
    for mark in marks:
        boundary = boundary + (position == mark).astype(jnp.int32)
    return jnp.cumsum(boundary, axis=1).astype(jnp.int32)


def levels(own_key, extent, shards, least, high):
    def one(axis_at, shards_of):
        steps = jax.random.uniform(jax.random.fold_in(jax.random.fold_in(own_key, 6), axis_at), (shards_of,), jnp.float32, least / len(shards), high / len(shards))
        return jnp.repeat(jnp.exp(steps), extent[axis_at] // shards_of).reshape((-1,) + (1,) * (len(extent) - axis_at - 1))

    factor_of = one(*shards[0])
    for cut in shards[1:]:
        factor_of = factor_of * one(*cut)
    return factor_of


def shared_out(rng, own, number, rows, count, top, reach, skew):
    order = jax.random.permutation(rng, count)
    packed, common = portions_of(count, rows * top, reach, skew, True), portions_of(count, rows * top, reach, skew, False)
    places = jnp.arange(count)

    def named(tallies, offset_by):
        used = int((tallies > 0).sum())
        fixed = max(1, used // 4)
        shifted = fixed + (places - fixed + offset_by * (used - fixed)) % max(1, count - fixed)
        return jnp.zeros((count,), jnp.int32).at[order[jnp.where(places < fixed, places, shifted)]].set(jnp.asarray(tallies, jnp.int32))

    tallies = jnp.where(number % 4 == 0, named(packed, number // 4), named(common, number - number // 4 - 1))
    mixed = jax.random.permutation(jax.random.fold_in(own, 3), count)
    source_of, receiver = mixed[0:count // 2 * 2:2], mixed[1:count // 2 * 2:2]
    margin = jnp.minimum(tallies[source_of] - 1, reach - tallies[receiver]) // 2
    margin = jnp.where((source_of == order[0]) | (receiver == order[0]) | (tallies[receiver] == 0), 0, jnp.maximum(margin, 0))
    shifted = jax.random.randint(jax.random.fold_in(own, 4), (count // 2,), 0, 1 << 20) % (margin + 1)
    tallies = tallies.at[source_of].add(-shifted).at[receiver].add(shifted)
    items = jnp.searchsorted(jnp.cumsum(tallies), jnp.arange(rows * top), side="right").astype(jnp.int32)
    table = items.reshape(top, rows).T
    table = table[jax.random.permutation(jax.random.fold_in(own, 1), rows)]
    offset_by = jax.random.randint(jax.random.fold_in(own, 2), (rows, 1), 0, top)
    return jnp.take_along_axis(table, (jnp.arange(top)[None, :] + offset_by) % top, axis=1)


def portions_of(amount, total, most, lean, full):
    weights = [(1 << 20) // math.isqrt(grade ** lean) + 1 for grade in range(1, amount + 1)]
    largest = most if full else min(most, max(-(-total // amount), total * weights[0] // sum(weights)))
    least = 1 if total - largest >= amount - 1 else 0
    counts, spare = [largest] + [least] * (amount - 1), total - largest - least * (amount - 1)
    while spare > 0:
        movable = [i for i in range(1, amount) if counts[i] < largest] or [i for i in range(1, amount) if counts[i] < most]
        mass, budget = sum([weights[i] for i in movable]), spare
        for i in movable:
            more = min(most - counts[i], max(1, budget * weights[i] // mass), spare)
            counts[i] = counts[i] + more
            spare = spare - more
    return np.array(counts)


def normal_values(own_key, extent, scale, reach, cuts=(), held_as=jnp.bfloat16):
    values = jax.random.normal(own_key, extent, jnp.float32) * scale
    if len(cuts) > 0:
        values = levels(own_key, extent, cuts, -0.22, 0.18) * values
    return jnp.clip(values, min=-reach, max=reach).astype(held_as)


def setup_inputs(seed: int = 0) -> dict:
    key_of = jax.random.split(jax.random.key(seed), 15)
    tokens = normal_values(key_of[0], (SEQS, LENGTH, D), 1.0, 6.0, ((0, 8), (1, 4)))
    segments = draw_segments(jax.random.fold_in(key_of[14], 71), 0)
    routes_keys = jax.random.split(jax.random.fold_in(key_of[2], 1), TOKENS // TOK_DEV)
    routes_turns = jax.random.permutation(jax.random.fold_in(key_of[2], 3), TOKENS // TOK_DEV)
    routes = jax.vmap(lambda own, number: shared_out(jax.random.fold_in(key_of[2], 2), own, number, TOK_DEV, EXPERTS, 1, CAP, 2))(routes_keys, routes_turns).reshape((TOKENS, 1))
    w_qkv = normal_values(key_of[3], (D, 3 * D), D ** -0.5, 0.1875)
    w_out = normal_values(key_of[4], (D, D), (D // 32) ** -0.5, 1.0)
    w_fc1 = normal_values(key_of[5], (D, FF), D ** -0.5, 0.1875)
    w_fc2 = normal_values(key_of[6], (FF, D), (FF // 4) ** -0.5, 0.1875)
    router = normal_values(key_of[7], (D, EXPERTS), (4 * D) ** -0.5, 0.09375)
    mix_weight = normal_values(key_of[8], (D, 2), D ** -0.5, 0.1875)
    gain_one = jnp.clip(1.0 + 0.1 * jax.random.normal(key_of[9], (D,), jnp.float32), 0.5, 1.5).astype(jnp.bfloat16)
    gain_two = jnp.clip(1.0 + 0.1 * jax.random.normal(key_of[10], (D,), jnp.float32), 0.5, 1.5).astype(jnp.bfloat16)
    expert_in = normal_values(key_of[11], (EXPERTS, D, FF), D ** -0.5, 0.1875, ((0, 8),))
    expert_out = normal_values(key_of[12], (EXPERTS, FF, D), (max(1, FF // (2 * EXPERTS * EXPERTS))) ** -0.5, 1.0, ((0, 8),))
    cotangent = normal_values(key_of[13], (SEQS, LENGTH, D), 1.0, 6.0, ((0, 8), (1, 4)))
    return {"tokens": tokens, "segments": segments, "routes": routes, "w_qkv": w_qkv, "w_out": w_out, "w_fc1": w_fc1, "w_fc2": w_fc2, "router": router, "mix_weight": mix_weight, "gain_one": gain_one, "gain_two": gain_two, "expert_in": expert_in, "expert_out": expert_out, "cotangent": cotangent}


@jax.custom_vjp
def low(v):
    return lax.optimization_barrier(v.astype(jnp.bfloat16)).astype(jnp.float32)

@jax.custom_vjp
def low_back(v):
    return v

def low_keep(v):
    return (low(v), None)

def low_pass(kept, grad):
    return (grad,)

def back_keep(v):
    return (v, None)

def back_low(kept, grad):
    return (low(grad),)
low.defvjp(low_keep, low_pass)
low_back.defvjp(back_keep, back_low)
EPSILON = 1e-05
NEGATIVE_FILL = -1e+30

def product(left, right):
    return jnp.dot(left, right, precision=lax.Precision.HIGHEST)

def normalize(values, gain):
    centred = values - lax.optimization_barrier(jnp.mean(values, axis=-1, keepdims=True))
    spread = lax.rsqrt(lax.optimization_barrier(jnp.mean(centred * centred, axis=-1, keepdims=True)) + EPSILON)
    return centred * spread * gain

def smooth(values):
    return jax.nn.gelu(values, approximate=True)

def layer_one(params, inputs):
    w_qkv, w_out, w_fc1, w_fc2, router, mix_weight, gain_one, gain_two, expert_in, expert_out = params
    sequence, segment, route = inputs
    length_all = sequence.shape[0]
    first = low(normalize(sequence, gain_one))
    projected = product(first, w_qkv)
    queries = low_back(low(projected[:, :D])).reshape(length_all, HEADS, HEAD_DIM)
    keys_all = low_back(low(projected[:, D:2 * D])).reshape(length_all, HEADS, HEAD_DIM)
    values_all = low_back(low(projected[:, 2 * D:])).reshape(length_all, HEADS, HEAD_DIM)
    scores = low_back(jnp.einsum('qhd,khd->hqk', queries, keys_all, precision=lax.Precision.HIGHEST) * HEAD_DIM ** (-0.5))
    position = jnp.arange(length_all)
    allowed = (position[None, :] <= position[:, None]) & (segment[None, :] == segment[:, None])
    probs = low(jax.nn.softmax(jnp.where(allowed[None], scores, NEGATIVE_FILL), axis=-1))
    attended = jnp.einsum('hqk,khd->qhd', probs, values_all, precision=lax.Precision.HIGHEST)
    attended = low_back(low(attended.reshape(length_all, D)))
    mid = sequence + low_back(product(attended, w_out))
    second = low(normalize(mid, gain_two))
    dense_hidden = low(smooth(low_back(product(second, w_fc1))))
    dense_result = low_back(product(dense_hidden, w_fc2))
    route_probs = jax.nn.softmax(low_back(product(second, router)), axis=-1)
    onehot = (route[:, None] == jnp.arange(EXPERTS)[None, :]).astype(jnp.float32)
    gate = lax.optimization_barrier(jnp.sum(route_probs * onehot, axis=-1, keepdims=True))
    mixing = jax.nn.softmax(low_back(product(second, mix_weight)), axis=-1)
    dispatched = low_back(second)

    def one_expert(total, members):
        weight_in, weight_back, column = members
        hidden = low(smooth(low_back(product(dispatched, weight_in))))
        produced = low_back(low(product(hidden, weight_back)))
        return (total + produced * column[:, None], None)
    expert_result = lax.scan(jax.checkpoint(one_expert), jnp.zeros_like(sequence), (expert_in, expert_out, onehot.T))[0]
    return mid + mixing[:, 0:1] * dense_result + mixing[:, 1:2] * gate * expert_result

def forward(params, inputs, segments, route_grid):

    def one_sequence(members):
        return layer_one(params, members)
    return lax.map(jax.checkpoint(one_sequence), (inputs, segments, route_grid))

def reference(tokens, segments, routes, w_qkv, w_out, w_fc1, w_fc2, router, mix_weight, gain_one, gain_two, expert_in, expert_out, cotangent):
    route_grid = routes.reshape(N_NARROW, N_WIDE, SEQ_W, LEN_DEV).transpose(1, 2, 0, 3).reshape(SEQS, LENGTH).astype(jnp.int32)
    params = tuple((member.astype(jnp.float32) for member in (w_qkv, w_out, w_fc1, w_fc2, router, mix_weight, gain_one, gain_two, expert_in, expert_out)))

    def whole(weights, inputs):
        return forward(weights, inputs, segments, route_grid)
    result, pullback = jax.vjp(whole, params, tokens.astype(jnp.float32))
    grads, input_grad = pullback(cotangent.astype(jnp.float32))
    return (result.astype(jnp.bfloat16), input_grad, grads[0], grads[1], grads[2], grads[3], grads[4], grads[5], grads[6], grads[7], grads[8], grads[9])
```

```python
import functools

import jax
import jax.numpy as jnp
from jax import lax
from jax.experimental import pallas as pl
from jax.experimental.pallas import tpu as pltpu
from jax.sharding import PartitionSpec as P

HEAD_DIM = 64
PAIR = 2 * HEAD_DIM
EPSILON = 1e-05
NEGATIVE_FILL = -1e30
VMEM_BYTES = 56 * 1024 * 1024
BF16 = jnp.bfloat16
F32 = jnp.float32


def normalize(values, gain):
    centred = values - jnp.mean(values, axis=-1, keepdims=True)
    spread = lax.rsqrt(jnp.mean(centred * centred, axis=-1, keepdims=True) + EPSILON)
    scaled = centred * spread
    return (scaled * gain, scaled, spread)


def normal_back(incoming, scaled, spread, gain):
    inner = incoming * gain
    return spread * (
        inner
        - jnp.mean(inner, axis=-1, keepdims=True)
        - scaled * jnp.mean(inner * scaled, axis=-1, keepdims=True)
    )


def dot(left, right, left_dim, right_dim):
    return lax.dot_general(
        left, right, (((left_dim,), (right_dim,)), ((), ())), preferred_element_type=F32
    )


def plain(left, right):
    return dot(left, right, 1, 0)


def across(left, right):
    return dot(left, right, 0, 0)


def beside(left, right):
    return dot(left, right, 1, 1)


def swap(values, axis, bit):
    size = lax.axis_size(axis)
    return lax.ppermute(values, axis, [(i, i ^ bit) for i in range(size)])


def x_bits():
    bits, bit = [], 2
    while bit < lax.axis_size("narrow"):
        bits.append(bit)
        bit *= 2
    return bits


def gather_pieces(values):
    pieces = [values]
    for bit in x_bits():
        pieces = pieces + [swap(piece, "narrow", bit) for piece in pieces]
    return pieces + [swap(piece, "narrow", 1) for piece in pieces]


def add_to_bf16(left, right):
    return (left.astype(F32) + right.astype(F32)).astype(BF16)


def scatter_addends(mine, other, rows):
    arrived = swap(other, "narrow", 1)
    bits = list(reversed(x_bits()))
    for bit in bits:
        half = mine.shape[0] // 2
        gone = add_to_bf16(mine[half:], arrived[half:])
        if bit == bits[-1]:
            return [mine, arrived, swap(gone, "narrow", bit)]
        mine, arrived = add_to_bf16(mine[:half], arrived[:half]), swap(gone, "narrow", bit)
    return [mine, arrived]


def natural_block(ids_ref, place, count):
    spots = count // 2
    return ids_ref[0] ^ (2 * (place % spots) + place // spots)


def natural_rows(ids_ref, place, count, rows):
    return pl.ds(pl.multiple_of(natural_block(ids_ref, place, count) * rows, rows), rows)


def params(steps=0):
    if steps:
        return pltpu.CompilerParams(
            vmem_limit_bytes=VMEM_BYTES, dimension_semantics=("arbitrary",) * steps
        )
    return pltpu.CompilerParams(vmem_limit_bytes=VMEM_BYTES)


def cost(flops, moved, curves=0):
    return pl.CostEstimate(flops=flops, bytes_accessed=moved, transcendentals=curves)


def in_vmem():
    return pl.BlockSpec(memory_space=pltpu.VMEM)


def in_smem():
    return pl.BlockSpec(memory_space=pltpu.SMEM)


def heads_kernel(ids_ref, *refs):
    *piece_refs, weight_ref, out_ref = refs
    count, rows = len(piece_refs), piece_refs[0].shape[0]
    for place, piece_ref in enumerate(piece_refs):
        out_ref[natural_rows(ids_ref, place, count, rows), :] = plain(
            piece_ref[...], weight_ref[...]
        ).astype(BF16)


def to_heads(ids, pieces, w_qkv):
    count = len(pieces)
    rows, width = pieces[0].shape
    part = width // count
    whole = pl.BlockSpec((rows, width), lambda j, s: (0, 0))
    return pl.pallas_call(
        heads_kernel,
        grid_spec=pltpu.PrefetchScalarGridSpec(
            num_scalar_prefetch=1,
            grid=(3,),
            in_specs=[whole] * count
            + [pl.BlockSpec((width, part), lambda j, s: (0, j * count + s[0]))],
            out_specs=pl.BlockSpec((count * rows, part), lambda j, s: (0, j)),
        ),
        out_shape=jax.ShapeDtypeStruct((count * rows, 3 * part), BF16),
        compiler_params=params(1),
        cost_estimate=cost(6 * count * rows * width * part, 2 * width * (count * rows + 3 * part)),
        name="to_heads",
    )(ids, *pieces, w_qkv)


def from_heads_kernel(count, ids_ref, d_ref, *refs):
    *weight_refs, mine_ref, other_ref = refs
    rows = d_ref.shape[0] // count
    weight = jnp.concatenate([ref[...] for ref in weight_refs], axis=1)
    for place in range(count):
        result = beside(d_ref[natural_rows(ids_ref, place, count, rows), :], weight)
        into = mine_ref if place < count // 2 else other_ref
        at = (place % (count // 2)) * rows
        into[at : at + rows, :] = result.astype(BF16)


def from_heads(ids, d_qkv, w_qkv):
    count = lax.axis_size("narrow")
    length, width = d_qkv.shape[0], w_qkv.shape[0]
    part = width // count
    half = pl.BlockSpec((length // 2, width), lambda i, s: (0, 0))
    place = lambda j: (lambda i, s: (0, j * count + s[0]))
    return pl.pallas_call(
        functools.partial(from_heads_kernel, count),
        grid_spec=pltpu.PrefetchScalarGridSpec(
            num_scalar_prefetch=1,
            grid=(1,),
            in_specs=[pl.BlockSpec(d_qkv.shape, lambda i, s: (0, 0))]
            + [pl.BlockSpec((width, part), place(j)) for j in range(3)],
            out_specs=[half, half],
        ),
        out_shape=[jax.ShapeDtypeStruct((length // 2, width), BF16)] * 2,
        compiler_params=params(1),
        cost_estimate=cost(6 * length * width * part, 2 * length * width * 2),
        name="from_heads",
    )(ids, d_qkv, w_qkv, w_qkv, w_qkv)


def block_bias(seg_row_ref, seg_col_ref, block, rows):
    keys = (block + 1) * rows
    key_pos = lax.broadcasted_iota(jnp.int32, (keys, rows), 0)
    query_pos = lax.broadcasted_iota(jnp.int32, (keys, rows), 1) + block * rows
    same = seg_col_ref[0:keys, :] == seg_row_ref[:, block * rows : (block + 1) * rows]
    return jnp.where((key_pos <= query_pos) & same, 0.0, NEGATIVE_FILL)


def soft_columns(keys, query, bias):
    scores = beside(keys, query) * (HEAD_DIM**-0.5) + bias
    weights = jnp.exp(scores - jnp.max(scores, axis=0, keepdims=True))
    return weights * (1.0 / jnp.sum(weights, axis=0, keepdims=True))


def attend_kernel(count, seg_row_ref, seg_col_ref, qkv_ref, out_ref):
    width = out_ref.shape[1]
    rows = out_ref.shape[0] // count
    lane = lax.broadcasted_iota(jnp.int32, (rows, PAIR), 1)
    for block in range(count):
        span = slice(block * rows, (block + 1) * rows)
        seen = slice(0, (block + 1) * rows)
        bias = block_bias(seg_row_ref, seg_col_ref, block, rows)
        for pair in range(width // PAIR):
            columns = slice(pair * PAIR, (pair + 1) * PAIR)
            query = qkv_ref[span, columns]
            keys = qkv_ref[seen, width + pair * PAIR : width + (pair + 1) * PAIR]
            values = qkv_ref[seen, 2 * width + pair * PAIR : 2 * width + (pair + 1) * PAIR]
            halves = []
            for head in range(2):
                here = (lane // HEAD_DIM) == head
                probs = soft_columns(keys, jnp.where(here, query, 0), bias).astype(BF16)
                mixed = across(values, probs)
                halves.append(mixed[head * HEAD_DIM : (head + 1) * HEAD_DIM])
            out_ref[span, columns] = jnp.concatenate(halves, axis=0).T.astype(BF16)


def attend_back_kernel(count, seg_row_ref, seg_col_ref, qkv_ref, d_ref, out_ref, total_ref):
    width = d_ref.shape[1]
    rows = d_ref.shape[0] // count
    scale = HEAD_DIM**-0.5
    lane = lax.broadcasted_iota(jnp.int32, (rows, PAIR), 1)
    total_ref[...] = jnp.zeros_like(total_ref)
    for block in range(count):
        span = slice(block * rows, (block + 1) * rows)
        seen = slice(0, (block + 1) * rows)
        bias = block_bias(seg_row_ref, seg_col_ref, block, rows)
        for pair in range(width // PAIR):
            columns = slice(pair * PAIR, (pair + 1) * PAIR)
            key_columns = slice(width + pair * PAIR, width + (pair + 1) * PAIR)
            value_columns = slice(2 * width + pair * PAIR, 2 * width + (pair + 1) * PAIR)
            query = qkv_ref[span, columns]
            keys = qkv_ref[seen, key_columns]
            values = qkv_ref[seen, value_columns]
            incoming = d_ref[span, columns]
            halves = []
            for head in range(2):
                here = (lane // HEAD_DIM) == head
                own_query = jnp.where(here, query, 0)
                own_incoming = jnp.where(here, incoming, 0)
                probs = soft_columns(keys, own_query, bias)
                d_probs = beside(values, own_incoming)
                mean = jnp.sum(probs * d_probs, axis=0, keepdims=True)
                d_scores = (probs * (d_probs - mean)).astype(BF16)
                total_ref[seen, width + pair * PAIR : width + (pair + 1) * PAIR] += plain(
                    probs.astype(BF16), own_incoming
                )
                total_ref[seen, columns] += plain(d_scores, own_query)
                mixed = across(keys, d_scores)
                halves.append(mixed[head * HEAD_DIM : (head + 1) * HEAD_DIM])
            out_ref[span, columns] = (jnp.concatenate(halves, axis=0).T * scale).astype(BF16)
    out_ref[:, width : 2 * width] = (total_ref[:, :width] * scale).astype(BF16)
    out_ref[:, 2 * width :] = total_ref[:, width:].astype(BF16)


def attention_cost(length, width, matmuls):
    return cost(
        matmuls * length * length * width,
        length * width * 16,
        length * length * width // HEAD_DIM,
    )


def attend(seg_row, seg_col, qkv):
    length, width = qkv.shape[0], qkv.shape[1] // 3
    return pl.pallas_call(
        functools.partial(attend_kernel, lax.axis_size("narrow")),
        out_shape=jax.ShapeDtypeStruct((length, width), BF16),
        in_specs=[in_vmem()] * 3,
        out_specs=in_vmem(),
        compiler_params=params(),
        cost_estimate=attention_cost(length, width, 4),
        name="attend",
    )(seg_row, seg_col, qkv)


def attend_back(seg_row, seg_col, qkv, d_attended):
    length, width = d_attended.shape
    return pl.pallas_call(
        functools.partial(attend_back_kernel, lax.axis_size("narrow")),
        out_shape=jax.ShapeDtypeStruct(qkv.shape, BF16),
        in_specs=[in_vmem()] * 4,
        out_specs=in_vmem(),
        scratch_shapes=[pltpu.VMEM((length, 2 * width), F32)],
        compiler_params=params(),
        cost_estimate=attention_cost(length, width, 10),
        name="attend_back",
    )(seg_row, seg_col, qkv, d_attended)


def softmax_lanes(logits, here):
    weights = jnp.where(here, jnp.exp(logits - jnp.max(jnp.where(here, logits, NEGATIVE_FILL), axis=-1, keepdims=True)), 0.0)
    return weights * (1.0 / jnp.sum(weights, axis=-1, keepdims=True))


def norm_rows(values):
    centred = values - jnp.mean(values, axis=-1, keepdims=True)
    spread = lax.rsqrt(jnp.mean(centred * centred, axis=-1, keepdims=True) + EPSILON)
    return (centred * spread, spread)


def pick(gates, lane, index):
    return jnp.sum(jnp.where(lane == index, gates, 0.0), axis=-1, keepdims=True)


def middle_kernel(
    experts,
    capacity,
    parts_ref,
    w_out_ref,
    tokens_ref,
    d_ref,
    gain_ref,
    logit_ref,
    routes_ref,
    mid_ref,
    second_ref,
    d_dense_ref,
    slots_ref,
    d_slots_ref,
    to_slot_ref,
    gates_ref,
):
    count, rows, part = parts_ref.shape
    attended = jnp.concatenate([parts_ref[k] for k in range(count)], axis=1)
    mid = tokens_ref[...].astype(F32) + plain(attended, w_out_ref[...])
    mid_ref[...] = mid
    second = (norm_rows(mid)[0] * gain_ref[...].astype(F32)).astype(BF16)
    second_ref[...] = second
    logits = plain(second, logit_ref[...])
    lane = lax.broadcasted_iota(jnp.int32, logits.shape, 1)
    route_probs = softmax_lanes(logits, lane < experts)
    mixing = softmax_lanes(logits, (lane >= experts) & (lane < experts + 2))
    gates_ref[...] = route_probs + mixing
    routes = routes_ref[...]
    chosen = lane == routes
    gate = jnp.sum(jnp.where(chosen, route_probs, 0.0), axis=-1, keepdims=True)
    d_output = d_ref[...].astype(F32)
    d_dense_ref[...] = (d_output * pick(mixing, lane, experts)).astype(BF16)
    d_expert = (d_output * pick(mixing, lane, experts + 1) * gate).astype(BF16)
    before = (
        lax.broadcasted_iota(jnp.int32, (rows, rows), 1)
        < lax.broadcasted_iota(jnp.int32, (rows, rows), 0)
    ).astype(F32).astype(BF16)
    earlier = plain(before, chosen.astype(F32).astype(BF16))
    position = jnp.sum(jnp.where(chosen, earlier, 0.0), axis=-1, keepdims=True)
    slot = routes * capacity + position.astype(jnp.int32)
    slots = experts * capacity
    to_slot = (
        (lax.broadcasted_iota(jnp.int32, (rows, slots), 1) == slot).astype(F32).astype(BF16)
    )
    to_slot_ref[...] = to_slot
    slots_ref[...] = across(to_slot, second).astype(BF16)
    d_slots_ref[...] = across(to_slot, d_expert).astype(BF16)


def middle(parts, w_out, tokens, d_output, gain, logit_weight, routes, experts, capacity):
    rows, width = tokens.shape
    slots = experts * capacity
    lanes = logit_weight.shape[1]
    return pl.pallas_call(
        functools.partial(middle_kernel, experts, capacity),
        out_shape=[
            jax.ShapeDtypeStruct((rows, width), F32),
            jax.ShapeDtypeStruct((rows, width), BF16),
            jax.ShapeDtypeStruct((rows, width), BF16),
            jax.ShapeDtypeStruct((slots, width), BF16),
            jax.ShapeDtypeStruct((slots, width), BF16),
            jax.ShapeDtypeStruct((rows, slots), BF16),
            jax.ShapeDtypeStruct((rows, lanes), F32),
        ],
        in_specs=[in_vmem()] * 7,
        out_specs=[in_vmem()] * 7,
        compiler_params=params(),
        cost_estimate=cost(2 * rows * width * (width + 2 * slots), 2 * width * (width + 8 * rows)),
        name="middle",
    )(parts, w_out, tokens, d_output, gain, logit_weight, routes)


def merge_kernel(
    experts,
    results,
    back_ref,
    d_back_ref,
    to_slot_ref,
    gates_ref,
    routes_ref,
    mid_ref,
    second_ref,
    d_ref,
    gain_ref,
    logit_ref,
    w_out_ref,
    *refs,
):
    sums, outs = refs[: 2 * results], refs[2 * results :]
    output_ref, d_mid_ref, d_attn_ref, d_attended_ref, small_ref = outs
    to_slot = to_slot_ref[...]
    expert_result = plain(to_slot, back_ref[...])
    d_second = plain(to_slot, d_back_ref[...])
    dense_result = sums[0][...].astype(F32)
    for ref in sums[1:results]:
        dense_result = dense_result + ref[...].astype(F32)
    for ref in sums[results:]:
        d_second = d_second + ref[...].astype(F32)
    gates = gates_ref[...]
    lane = lax.broadcasted_iota(jnp.int32, gates.shape, 1)
    chosen = lane == routes_ref[...]
    gate = pick(gates, lane, routes_ref[...])
    mix_dense, mix_expert = pick(gates, lane, experts), pick(gates, lane, experts + 1)
    mid = mid_ref[...]
    d_output = d_ref[...].astype(F32)
    output_ref[...] = (
        mid + mix_dense * dense_result + mix_expert * gate * expert_result
    ).astype(BF16)
    on_dense = jnp.sum(d_output * dense_result, axis=-1, keepdims=True)
    on_expert = jnp.sum(d_output * expert_result, axis=-1, keepdims=True)
    mean = mix_dense * on_dense + mix_expert * (gate * on_expert)
    d_mix = gates * (jnp.where(lane == experts, on_dense, gate * on_expert) - mean)
    d_route = gates * (chosen.astype(F32) - gate) * (mix_expert * on_expert)
    d_logits = jnp.where(
        lane < experts, d_route, jnp.where(lane < experts + 2, d_mix, 0.0)
    ).astype(BF16)
    d_second = d_second + beside(d_logits, logit_ref[...])
    scaled, spread = norm_rows(mid)
    d_gain = jnp.sum(d_second * scaled, axis=0, keepdims=True)
    d_mid = d_output + normal_back(d_second, scaled, spread, gain_ref[...].astype(F32))
    d_mid_ref[...] = d_mid
    d_attn = d_mid.astype(BF16)
    d_attended = beside(d_attn, w_out_ref[...]).astype(BF16)
    count, rows, part = d_attn_ref.shape
    for block in range(count):
        d_attn_ref[block] = d_attn[:, block * part : (block + 1) * part]
        d_attended_ref[block] = d_attended[:, block * part : (block + 1) * part]
    small = across(second_ref[...], d_logits)
    column = jnp.broadcast_to(d_gain, (small.shape[1], small.shape[0])).T
    small_lane = lax.broadcasted_iota(jnp.int32, small.shape, 1)
    small_ref[...] = jnp.where(small_lane == experts + 2, column, small).astype(BF16)


def merge(back, d_back, to_slot, gates, routes, mid, second, d_output, gain, logit_weight, w_out,
          dense_sums, d_second_sums, experts, count):
    rows, width = mid.shape
    part = width // count
    slots = to_slot.shape[1]
    lanes = logit_weight.shape[1]
    whole = lambda v: pl.BlockSpec(v.shape, lambda i: (0,) * v.ndim)
    top = pl.BlockSpec((rows, width), lambda i: (0, 0))
    blocks = pl.BlockSpec((count, rows, part), lambda i: (0, 0, 0))
    given = (back, d_back, to_slot, gates, routes, mid, second, d_output, gain, logit_weight, w_out)
    return pl.pallas_call(
        functools.partial(merge_kernel, experts, len(dense_sums)),
        grid=(1,),
        out_shape=[
            jax.ShapeDtypeStruct((rows, width), BF16),
            jax.ShapeDtypeStruct((rows, width), F32),
            jax.ShapeDtypeStruct((count, rows, part), BF16),
            jax.ShapeDtypeStruct((count, rows, part), BF16),
            jax.ShapeDtypeStruct((width, lanes), BF16),
        ],
        in_specs=[whole(v) for v in given] + [top] * (2 * len(dense_sums)),
        out_specs=[top, top, blocks, blocks, pl.BlockSpec((width, lanes), lambda i: (0, 0))],
        compiler_params=params(1),
        cost_estimate=cost(2 * rows * width * (width + 2 * slots), 2 * width * (width + 16 * rows)),
        name="merge",
    )(*given, *dense_sums, *d_second_sums)


def finish_kernel(tokens_ref, gain_ref, d_mid_ref, *refs):
    *sum_refs, out_ref = refs
    incoming = sum_refs[0][...].astype(F32)
    for ref in sum_refs[1:]:
        incoming = incoming + ref[...].astype(F32)
    scaled, spread = norm_rows(tokens_ref[...].astype(F32))
    out_ref[...] = d_mid_ref[...] + normal_back(
        incoming, scaled, spread, gain_ref[...].astype(F32)
    )


def finish(tokens, gain, d_mid, sums):
    rows, width = tokens.shape
    top = pl.BlockSpec((rows, width), lambda i: (0, 0))
    return pl.pallas_call(
        finish_kernel,
        grid=(1,),
        out_shape=jax.ShapeDtypeStruct((rows, width), F32),
        in_specs=[top, pl.BlockSpec((1, width), lambda i: (0, 0)), top] + [top] * len(sums),
        out_specs=top,
        compiler_params=params(1),
        cost_estimate=cost(20 * rows * width, 20 * rows * width),
        name="finish",
    )(tokens, gain, d_mid, *sums)


def whole_rows(refs):
    return jnp.concatenate([ref[...] for ref in refs], axis=0)


def whole_columns(refs):
    return jnp.concatenate([ref[...] for ref in refs], axis=1)


def row_chunks(refs, size):
    chunks, at = [], 0
    for ref in refs:
        for start in range(0, ref.shape[0], size):
            chunks.append((ref, start, at + start))
        at += ref.shape[0]
    return chunks


CHUNK = 256


def write_halves(total_ref, mine_ref, other_ref):
    @pl.when(pl.program_id(0) == pl.num_programs(0) - 1)
    def _():
        half = mine_ref.shape[0]
        mine_ref[...] = total_ref[:half, :].astype(BF16)
        other_ref[...] = total_ref[half:, :].astype(BF16)


def clear_first(total_ref):
    @pl.when(pl.program_id(0) == 0)
    def _():
        total_ref[...] = jnp.zeros_like(total_ref)


def forward_kernel(pieces, slices, ids_ref, *refs):
    piece_refs, refs = refs[:pieces], refs[pieces:]
    in_refs, out_refs, refs = refs[:slices], refs[slices : 2 * slices], refs[2 * slices :]
    hidden_ref, slope_ref, mine_ref, other_ref, total_ref = refs
    clear_first(total_ref)
    weight_in, weight_out = whole_columns(in_refs), whole_rows(out_refs)
    chunks = row_chunks(piece_refs, CHUNK)
    first_dot = lambda c: plain(c[0][c[1] : c[1] + CHUNK, :], weight_in)
    pre = first_dot(chunks[0])
    for index, (_, _, at) in enumerate(chunks):
        later = first_dot(chunks[index + 1]) if index + 1 < len(chunks) else None
        square = pre * pre
        curve = jnp.tanh(pre * (0.7978845608 + (0.7978845608 * 0.044715) * square))
        half = 0.5 + 0.5 * curve
        hidden = (pre * half).astype(BF16)
        slope = half + (0.5 * pre) * (1.0 - curve * curve) * (
            0.7978845608 + (3.0 * 0.7978845608 * 0.044715) * square
        )
        hidden_ref[at : at + CHUNK, :] = hidden
        slope_ref[at : at + CHUNK, :] = slope.astype(BF16)
        total_ref[at : at + CHUNK, :] += plain(hidden, weight_out)
        pre = later
    write_halves(total_ref, mine_ref, other_ref)


def backward_kernel(pieces, slices, ids_ref, *refs):
    piece_refs, refs = refs[:pieces], refs[pieces:]
    in_refs, out_refs, refs = refs[:slices], refs[slices : 2 * slices], refs[2 * slices :]
    slope_ref, d_pre_ref, mine_ref, other_ref, total_ref = refs
    clear_first(total_ref)
    weight_in, weight_out = whole_columns(in_refs), whole_rows(out_refs)
    chunks = row_chunks(piece_refs, CHUNK)
    first_dot = lambda c: beside(c[0][c[1] : c[1] + CHUNK, :], weight_out)
    d_hidden = first_dot(chunks[0])
    for index, (_, _, at) in enumerate(chunks):
        later = first_dot(chunks[index + 1]) if index + 1 < len(chunks) else None
        d_pre = (d_hidden * slope_ref[at : at + CHUNK, :].astype(F32)).astype(BF16)
        d_pre_ref[at : at + CHUNK, :] = d_pre
        total_ref[at : at + CHUNK, :] += beside(d_pre, weight_in)
        d_hidden = later
    write_halves(total_ref, mine_ref, other_ref)


def feed(kernel, name, ids, pieces, weight_in, weight_out, units, places, block, slope=None):
    width = pieces[0].shape[1]
    count = sum(piece.shape[0] for piece in pieces)
    size = block // len(places)
    unit_spec = pl.BlockSpec((count, block), lambda f, s: (0, f))
    half_spec = pl.BlockSpec((count // 2, width), lambda f, s: (0, 0))
    in_places = [(lambda f, s, p=p: (0, p(f, s))) for p in places]
    out_places = [(lambda f, s, p=p: (p(f, s), 0)) for p in places]
    in_specs = (
        [pl.BlockSpec(piece.shape, lambda f, s: (0, 0)) for piece in pieces]
        + [pl.BlockSpec((width, size), p) for p in in_places]
        + [pl.BlockSpec((size, width), p) for p in out_places]
    )
    given = [*pieces] + [weight_in] * len(places) + [weight_out] * len(places)
    if slope is not None:
        in_specs.append(unit_spec)
        given.append(slope)
    unit_outs = 2 if slope is None else 1
    return pl.pallas_call(
        functools.partial(kernel, len(pieces), len(places)),
        grid_spec=pltpu.PrefetchScalarGridSpec(
            num_scalar_prefetch=1,
            grid=(units // block,),
            in_specs=in_specs,
            out_specs=[unit_spec] * unit_outs + [half_spec] * 2,
            scratch_shapes=[pltpu.VMEM((count, width), F32)],
        ),
        out_shape=[jax.ShapeDtypeStruct((count, units), BF16)] * unit_outs
        + [jax.ShapeDtypeStruct((count // 2, width), BF16)] * 2,
        compiler_params=params(1),
        cost_estimate=cost(
            4 * count * width * units,
            2 * (2 * count * width + 2 * width * units + 2 * count * units),
            count * units,
        ),
        name=name,
    )(ids, *given)


def grad_kernel(lefts, rights, ids_ref, *refs):
    left = whole_rows(refs[:lefts])
    right = whole_rows(refs[lefts : lefts + rights])
    total = across(left, right)
    for ref in refs[lefts + rights : -1]:
        total = total + ref[...].astype(F32)
    refs[-1][...] = total.astype(refs[-1].dtype)


def grad(name, ids, lefts, rights, rows, steps, left_place, columns=None, right_place=None,
         added=None, added_place=None, out=None, out_place=None, dtype=BF16):
    depth = sum(v.shape[0] for v in lefts)
    columns = columns or rights[0].shape[1]
    right_place = right_place or (lambda i, s: 0)
    out_place = out_place or (lambda i, s: (i, 0))
    out = out or (rows * steps, columns)
    in_specs = [
        pl.BlockSpec((v.shape[0], rows), lambda i, s: (0, left_place(i, s))) for v in lefts
    ] + [pl.BlockSpec((v.shape[0], columns), lambda i, s: (0, right_place(i, s))) for v in rights]
    given = [*lefts, *rights]
    if added is not None:
        in_specs.append(pl.BlockSpec((rows, columns), added_place or out_place))
        given.append(added)
    return pl.pallas_call(
        functools.partial(grad_kernel, len(lefts), len(rights)),
        grid_spec=pltpu.PrefetchScalarGridSpec(
            num_scalar_prefetch=1,
            grid=(steps,),
            in_specs=in_specs,
            out_specs=pl.BlockSpec((rows, columns), out_place),
        ),
        out_shape=jax.ShapeDtypeStruct(out, dtype),
        compiler_params=params(1),
        cost_estimate=cost(
            2 * depth * rows * steps * columns,
            2 * (depth * (rows * steps + columns) + 2 * rows * steps * columns),
        ),
        name=name,
    )(ids, *given)


def feed_grads_kernel(pieces, ids_ref, hidden_ref, d_pre_ref, *refs):
    row_refs, d_refs, (keep_ref, gone_ref) = refs[:pieces], refs[pieces:-2], refs[-2:]
    part = d_pre_ref.shape[1]
    half = keep_ref.shape[0]
    swapped = (ids_ref[3] & 1) == 1

    def put(total, columns):
        total = total.astype(BF16)
        keep_ref[:, columns] = jnp.where(swapped, total[half:], total[:half])
        gone_ref[:, columns] = jnp.where(swapped, total[:half], total[half:])

    put(across(whole_rows(row_refs), d_pre_ref[...]), slice(0, part))
    put(across(hidden_ref[...], whole_rows(d_refs)), slice(part, part + keep_ref.shape[1] - part))


def feed_grads(ids, rows, d_rows, hidden, d_pre):
    count, width = rows[0].shape
    length, part = d_pre.shape
    steps = lax.axis_size("wide") // 2
    fixed = lambda v: pl.BlockSpec(v.shape, lambda i, s: (0, 0))
    out = jax.ShapeDtypeStruct((width // 2, part + width), BF16)
    out_spec = pl.BlockSpec((width // steps // 2, part + width), lambda i, s: (i, 0))
    return pl.pallas_call(
        functools.partial(feed_grads_kernel, len(rows)),
        grid_spec=pltpu.PrefetchScalarGridSpec(
            num_scalar_prefetch=1,
            grid=(steps,),
            in_specs=[pl.BlockSpec((length, part // steps), lambda i, s: (0, i)), fixed(d_pre)]
            + [pl.BlockSpec((count, width // steps), lambda i, s: (0, i))] * len(rows)
            + [fixed(v) for v in d_rows],
            out_specs=[out_spec, out_spec],
        ),
        out_shape=[out, out],
        compiler_params=params(1),
        cost_estimate=cost(4 * length * width * part, 2 * (4 * length * width + 2 * width * part)),
        name="feed_grads",
    )(ids, hidden, d_pre, *rows, *d_rows)


def heads_grad_kernel(count, ids_ref, *refs):
    piece_refs, (d_ref, out_sum_ref, small_ref, out_ref) = refs[:count], refs[count:]
    rows = piece_refs[0].shape[0]
    right = jnp.concatenate(
        [d_ref[natural_rows(ids_ref, place, count, rows), :] for place in range(count)], axis=0
    )
    triple, part = right.shape[1], out_sum_ref.shape[1]
    out_ref[:, :triple] = across(whole_rows(piece_refs), right).astype(BF16)
    out_ref[:, triple : triple + part] = out_sum_ref[...]
    out_ref[:, triple + part :] = small_ref[...]


def heads_grad(ids, pieces, d_qkv, out_sum, small):
    rows, width = pieces[0].shape
    length, triple = d_qkv.shape
    part, lanes = out_sum.shape[1], small.shape[1]
    block = 256
    return pl.pallas_call(
        functools.partial(heads_grad_kernel, len(pieces)),
        grid_spec=pltpu.PrefetchScalarGridSpec(
            num_scalar_prefetch=1,
            grid=(width // block,),
            in_specs=[pl.BlockSpec((rows, block), lambda i, s: (0, i))] * len(pieces)
            + [
                pl.BlockSpec(d_qkv.shape, lambda i, s: (0, 0)),
                pl.BlockSpec((block, part), lambda i, s: (i, 0)),
                pl.BlockSpec((block, lanes), lambda i, s: (i, 0)),
            ],
            out_specs=pl.BlockSpec((block, triple + part + lanes), lambda i, s: (i, 0)),
        ),
        out_shape=jax.ShapeDtypeStruct((width, triple + part + lanes), BF16),
        compiler_params=params(1),
        cost_estimate=cost(2 * length * width * triple, 4 * length * width),
        name="heads_grad",
    )(ids, *pieces, d_qkv, out_sum, small)


def out_grad_kernel(ids_ref, attended_ref, d_ref, mine_ref, other_ref):
    count, _, part = d_ref.shape
    spots = count // 2
    for place in range(count):
        total = across(attended_ref[0], d_ref[natural_block(ids_ref, place, count)])
        into = mine_ref if place < spots else other_ref
        at = (place % spots) * part
        into[:, at : at + part] = total.astype(BF16)


def out_grad(ids, attended, d_attn):
    count, rows, part = attended.shape
    out = jax.ShapeDtypeStruct((count * part, count * part // 2), BF16)
    out_spec = pl.BlockSpec((part, count * part // 2), lambda i, s: (i, 0))
    return pl.pallas_call(
        out_grad_kernel,
        grid_spec=pltpu.PrefetchScalarGridSpec(
            num_scalar_prefetch=1,
            grid=(count,),
            in_specs=[
                pl.BlockSpec((1, rows, part), lambda i, s: (i, 0, 0)),
                pl.BlockSpec(d_attn.shape, lambda i, s: (0, 0, 0)),
            ],
            out_specs=[out_spec, out_spec],
        ),
        out_shape=[out, out],
        compiler_params=params(1),
        cost_estimate=cost(2 * rows * (part * count) ** 2, 8 * (part * count) ** 2),
        name="out_grad",
    )(ids, attended, d_attn)


def scatter_columns(mine, other, columns):
    total = add_to_bf16(mine, swap(other, "narrow", 1))
    for bit in reversed(x_bits()):
        half = total.shape[1] // 2
        total = add_to_bf16(total[:, :half], swap(total[:, half:], "narrow", bit))
    return total


def put_feed_kernel(count, all_ref, first_out_ref, second_out_ref):
    held, width = all_ref.shape[1], second_out_ref.shape[1]
    part = all_ref.shape[2] - width
    for n in range(count):
        for w in range(part // held):
            at = (w * count + n) * held
            first_out_ref[:, at : at + held] = all_ref[n][:, w * held : (w + 1) * held].astype(F32)
        second_out_ref[n * held : (n + 1) * held, :] = all_ref[n][:, part:].astype(F32)


def put_feed(feed_all, width):
    count, held, both = feed_all.shape
    part = both - width
    return pl.pallas_call(
        functools.partial(put_feed_kernel, count),
        out_shape=[
            jax.ShapeDtypeStruct((held, count * part), F32),
            jax.ShapeDtypeStruct((count * held, width), F32),
        ],
        in_specs=[in_vmem()],
        out_specs=[in_vmem()] * 2,
        compiler_params=params(),
        cost_estimate=cost(0, 6 * count * held * both),
        name="put_feed",
    )(feed_all)


def put_heads_kernel(count, experts, ids_ref, *refs):
    piece_refs, refs = refs[:count], refs[count:]
    w_ref, gain_ref, grad_qkv_ref, grad_out_ref, router_ref, mix_ref, one_ref, two_ref = refs
    width = w_ref.shape[1] // 3
    part = width // count
    small = None
    for place in range(count):
        n = natural_block(ids_ref, place, count)
        for j in range(3):
            at = pl.multiple_of(j * width + n * part, part)
            grad_qkv_ref[:, pl.ds(at, part)] = piece_refs[place][
                :, j * part : (j + 1) * part
            ].astype(F32)
        at = pl.multiple_of(n * part, part)
        grad_out_ref[:, pl.ds(at, part)] = piece_refs[place][:, 3 * part : 4 * part].astype(F32)
        its = piece_refs[place][:, 4 * part :].astype(F32)
        small = its if small is None else small + its
    router_ref[...] = small[:, :experts]
    mix_ref[...] = small[:, experts : experts + 2]
    two_ref[...] = small.T[experts + 2 : experts + 3, :]
    weighed = jnp.sum(w_ref[...].astype(F32) * grad_qkv_ref[...], axis=1, keepdims=True)
    weighed = jnp.broadcast_to(weighed, small.shape).T[0:1, :]
    one_ref[...] = weighed / gain_ref[0].astype(F32)


def put_heads(ids, pieces, w_qkv, gain, experts):
    count = len(pieces)
    held = pieces[0].shape[0]
    width = w_qkv.shape[0]
    fixed = lambda shape: pl.BlockSpec(shape, lambda i, s: (0,) * len(shape))
    outs = [(held, 3 * width), (held, width), (held, experts), (held, 2), (1, held), (1, held)]
    return pl.pallas_call(
        functools.partial(put_heads_kernel, count, experts),
        grid_spec=pltpu.PrefetchScalarGridSpec(
            num_scalar_prefetch=1,
            grid=(1,),
            in_specs=[fixed(v.shape) for v in pieces]
            + [
                pl.BlockSpec((held, 3 * width), lambda i, s: (s[3], 0)),
                pl.BlockSpec((1, 1, held), lambda i, s: (s[3], 0, 0)),
            ],
            out_specs=[fixed(shape) for shape in outs],
        ),
        out_shape=[jax.ShapeDtypeStruct(shape, F32) for shape in outs],
        compiler_params=params(1),
        cost_estimate=cost(2 * held * 3 * width, 20 * held * width),
        name="put_heads",
    )(ids, *pieces, w_qkv, gain.reshape(width // held, 1, held))


def fill_kernel(ids_ref, half_ref, whole_ref, out_ref):
    out_ref[...] = half_ref[...].astype(F32)


def fill_other(ids, half, whole):
    rows, columns = half.shape
    spots = lax.axis_size("narrow") // 2
    quarter = columns // spots
    return pl.pallas_call(
        fill_kernel,
        grid_spec=pltpu.PrefetchScalarGridSpec(
            num_scalar_prefetch=1,
            grid=(spots,),
            in_specs=[
                pl.BlockSpec((rows, quarter), lambda i, s: (0, i)),
                pl.BlockSpec(memory_space=pl.ANY),
            ],
            out_specs=pl.BlockSpec((rows, quarter), lambda i, s: (0, 2 * i + 1 - s[1])),
        ),
        out_shape=jax.ShapeDtypeStruct(whole.shape, F32),
        input_output_aliases={2: 0},
        compiler_params=params(1),
        cost_estimate=cost(0, 6 * rows * columns),
        name="fill_other",
    )(ids, half, whole)


def wide_sum(values):
    return lax.psum_scatter(values, "wide", scatter_dimension=0, tiled=True)


def wide_sum_at_once(values):
    wide = lax.axis_size("wide")
    blocks = values.reshape(wide, values.shape[0] // wide, values.shape[1])
    arrived = lax.all_to_all(blocks, "wide", split_axis=0, concat_axis=0, tiled=True)
    return jnp.sum(arrived.astype(F32), axis=0).astype(BF16)


def narrow_all(values):
    return lax.all_gather(values, "narrow", axis=0, tiled=False)


def tied(value, *others):
    return lax.optimization_barrier((value, *others))[0]


def out_leaves(ids, d_rows, hidden):
    block = min(512, hidden.shape[1] // 2)
    per = hidden.shape[1] // 2 // block
    return grad("out_gone", ids, [hidden], d_rows, block, per, lambda i, s: (1 - s[2]) * per + i)


def in_leaves(ids, rows, d_pre):
    part = rows[0].shape[1] // 4
    return grad("in_gone", ids, rows, [d_pre], part, 2, lambda i, s: 2 * (1 - s[2]) + i)


def expert_grads(ids, rows, d_rows, hidden, d_pre, own, out_came, in_came, later):
    narrow = lax.axis_size("narrow")
    spots = narrow // 2
    width, shared = rows[0].shape[1], hidden.shape[1]
    quarter = shared // spots
    part = width // narrow
    if spots == 2:
        block = min(512, quarter)
        per = quarter // block
        hidden = tied(hidden, later)
        grad_out = grad("out_kept", ids, [hidden], d_rows, block, per,
                        lambda i, s: s[2] * per + i, added=out_came, dtype=F32)
        in_other = grad("in_other", ids, rows, [d_pre], part, 1,
                        lambda i, s: 2 * s[2] + 1 - s[1], added=in_came,
                        added_place=lambda i, s: (1 - s[1], 0))
        in_arrived = swap(in_other, "narrow", 1)
        in_kept = grad("in_kept", ids, rows, [d_pre], part, spots,
                       lambda i, s: 2 * s[2] + s[1], columns=quarter,
                       right_place=lambda i, s: i, added=in_came,
                       added_place=lambda i, s: (s[1], i),
                       out=(part, 2 * shared), out_place=lambda i, s: (0, 2 * i + s[1]),
                       dtype=F32)
        return fill_other(ids, in_arrived, in_kept), grad_out
    groups = [[2 * x + c for x in range(spots)] for c in range(2)]
    all_rows = jnp.concatenate(rows, axis=0)
    all_d_rows = jnp.concatenate(d_rows, axis=0)
    over_x = lambda v: lax.psum_scatter(
        v.astype(BF16), "narrow", scatter_dimension=0, axis_index_groups=groups, tiled=True
    )
    grad_out = over_x(across(hidden, all_d_rows)).astype(F32)
    in_sum = over_x(across(all_rows, d_pre)).reshape(2, part, shared)
    core = own & 1
    kept = lax.dynamic_index_in_dim(in_sum, core, 0, keepdims=False).astype(F32)
    gone = lax.dynamic_index_in_dim(in_sum, 1 - core, 0, keepdims=False)
    came = swap(gone, "narrow", 1).astype(F32)
    even = jnp.where(core == 0, kept, came).reshape(part, spots, 1, quarter)
    odd = jnp.where(core == 0, came, kept).reshape(part, spots, 1, quarter)
    grad_in = jnp.concatenate([even, odd], axis=2).reshape(part, 2 * shared)
    return grad_in, grad_out


def per_device(
    tokens,
    segments,
    routes,
    w_qkv,
    w_out,
    w_fc1,
    w_fc2,
    router,
    mix_weight,
    gain_one,
    gain_two,
    expert_in,
    expert_out,
    cotangent,
):
    rows, width = tokens.shape[1:]
    length = segments.shape[1]
    experts = router.shape[1]
    capacity = 2 * rows // experts
    narrow, wide = lax.axis_size("narrow"), lax.axis_size("wide")
    own = lax.axis_index("narrow")
    units = w_fc1.shape[1]
    part = width // narrow
    ids = jnp.stack([own, own & 1, own >> 1, lax.axis_index("wide")]).astype(jnp.int32)
    seg_row, seg_col = segments.reshape(1, length), segments.reshape(length, 1)
    own_tokens, d_output = tokens[0], cotangent[0]
    gain_row_one, gain_row_two = gain_one.reshape(1, width), gain_two.reshape(1, width)
    lanes = -(-(experts + 3) // 128) * 128
    logit_weight = jnp.concatenate(
        [router, mix_weight, jnp.zeros((width, lanes - experts - 2), BF16)], axis=1
    )

    first = normalize(own_tokens.astype(F32), gain_one.astype(F32))[0].astype(BF16)
    first_pieces = gather_pieces(first)
    qkv = to_heads(ids, first_pieces, w_qkv)
    attended_part = attend(seg_row, seg_col, qkv)
    attended = lax.all_to_all(
        attended_part.reshape(narrow, rows, part), "narrow", split_axis=0, concat_axis=0, tiled=True
    )
    mid, second, d_dense, slots, d_slots, to_slot, gates = middle(
        attended, w_out, own_tokens, d_output, gain_row_two, logit_weight, routes, experts, capacity
    )

    def to_experts(values):
        values = values.reshape(experts, capacity, width)
        arrived = lax.all_to_all(values, "wide", split_axis=0, concat_axis=0, tiled=True)
        return arrived.reshape(experts * capacity, width)

    def to_tokens(both):
        both = both.reshape(experts, capacity, width)
        back = lax.all_to_all(both, "wide", split_axis=0, concat_axis=0, tiled=True)
        return back.reshape(experts * capacity, width)

    expert_rows = to_experts(slots)

    slot = units // (wide * narrow)
    dense_units = units // narrow
    dense_block = min(512, dense_units)
    if slot % 128 == 0:
        slices = dense_block // slot
        dense_places = [
            (lambda f, s, i=i: (f * slices + i) * narrow + s[0]) for i in range(slices)
        ]
        fc1_part, fc2_part = w_fc1, w_fc2
    else:
        dense_places = [lambda f, s: f]
        fc1_part = lax.dynamic_index_in_dim(
            w_fc1.reshape(width, wide, narrow, slot), own, 2, keepdims=False
        ).reshape(width, dense_units)
        fc2_part = lax.dynamic_index_in_dim(
            w_fc2.reshape(wide, narrow, slot, width), own, 1, keepdims=False
        ).reshape(dense_units, width)
    second_pieces = gather_pieces(second)
    d_dense_pieces = gather_pieces(d_dense)
    dense_hidden, dense_slope, dense_mine, dense_other = feed(
        forward_kernel, "dense_forward", ids, second_pieces, fc1_part, fc2_part,
        dense_units, dense_places, dense_block,
    )
    expert_rows = tied(expert_rows, dense_hidden)
    expert_d_rows = to_experts(tied(d_slots, expert_rows))
    expert_rows = [expert_rows, swap(expert_rows, "narrow", 1)]
    expert_d_rows = [expert_d_rows, swap(expert_d_rows, "narrow", 1)]
    dense_sums = scatter_addends(dense_mine, dense_other, rows)
    d_dense_pre, d_second_mine, d_second_other = feed(
        backward_kernel, "dense_backward", ids, d_dense_pieces, fc1_part, fc2_part,
        dense_units, dense_places, dense_block, dense_slope,
    )
    d_second_sums = scatter_addends(d_second_mine, d_second_other, rows)

    quarter = units // narrow
    expert_block = min(512, quarter)
    per_quarter = quarter // expert_block
    expert_places = [
        lambda f, s: (2 * (f // per_quarter) + s[1]) * per_quarter + f % per_quarter
    ]
    expert_rows = [tied(expert_rows[0], d_second_mine), expert_rows[1]]
    expert_hidden, expert_slope, produced_mine, produced_other = feed(
        forward_kernel, "expert_forward", ids, expert_rows, expert_in[0], expert_out[0],
        units // 2, expert_places, expert_block,
    )
    produced = add_to_bf16(produced_mine, swap(produced_other, "narrow", 1))
    back = to_tokens(produced)
    out_gone = out_leaves(ids, expert_d_rows, expert_hidden) if narrow == 4 else produced
    d_expert_pre, d_sent_mine, d_sent_other = feed(
        backward_kernel, "expert_backward", ids, expert_d_rows, expert_in[0], expert_out[0],
        units // 2, expert_places, expert_block, tied(expert_slope, out_gone, produced, dense_sums[-1], d_second_sums[-1]),
    )
    d_back = to_tokens(add_to_bf16(d_sent_mine, swap(d_sent_other, "narrow", 1)))
    dense_hidden = tied(dense_hidden, back, d_expert_pre)
    if slot % 128 == 0:
        feed_keep, feed_gone = feed_grads(
            ids, second_pieces, d_dense_pieces, dense_hidden, d_dense_pre
        )
    else:
        fc1_sum = wide_sum(
            grad("fc1_grad", ids, second_pieces, [d_dense_pre], 256, width // 256, lambda i, s: i)
        )
        fc2_sum = wide_sum(
            grad("fc2_grad", ids, [dense_hidden], d_dense_pieces, 256, dense_units // 256,
                 lambda i, s: i)
        )

    in_gone = in_leaves(ids, expert_rows, d_expert_pre) if narrow == 4 else d_back
    out_came, in_came = swap(out_gone, "narrow", 2), swap(in_gone, "narrow", 2)

    output, d_mid, d_attn, d_attended, small = merge(
        back, d_back, tied(to_slot, in_gone, out_came), gates, routes, mid, second, d_output, gain_row_two, logit_weight,
        w_out, dense_sums, d_second_sums, experts, narrow,
    )
    d_attended_part = lax.all_to_all(
        d_attended, "narrow", split_axis=0, concat_axis=0, tiled=True
    ).reshape(length, part)
    out_mine, out_other = out_grad(ids, attended, d_attn)
    out_sum = scatter_columns(out_mine, out_other, part)
    if slot % 128 == 0:
        feed_sum = lax.psum_scatter(
            add_to_bf16(tied(feed_keep, d_attended), swap(feed_gone, "wide", 1)),
            "wide",
            scatter_dimension=0,
            axis_index_groups=[[2 * z + y for z in range(wide // 2)] for y in range(2)],
            tiled=True,
        )
    d_qkv = attend_back(seg_row, seg_col, tied(qkv, out_mine), d_attended_part)
    d_first_mine, d_first_other = from_heads(ids, d_qkv, w_qkv)
    d_first_sums = scatter_addends(d_first_mine, d_first_other, rows)
    heads_sum = wide_sum_at_once(
        heads_grad(ids, first_pieces, tied(d_qkv, in_came), out_sum, small)
    )
    input_grad = finish(own_tokens, gain_row_one, d_mid, d_first_sums)
    grad_expert_in, grad_expert_out = expert_grads(
        ids, expert_rows, expert_d_rows, expert_hidden, d_expert_pre, own, out_came, in_came, d_qkv
    )

    held = width // wide
    if slot % 128 == 0:
        grad_fc1, grad_fc2 = put_feed(narrow_all(feed_sum), width)
    else:
        fc1_all, fc2_all = narrow_all(fc1_sum), narrow_all(fc2_sum)
        grad_fc1 = (
            fc1_all.reshape(narrow, held, wide, slot).transpose(1, 2, 0, 3).reshape(held, units)
        ).astype(F32)
        grad_fc2 = fc2_all.reshape(units // wide, width).astype(F32)
    grad_qkv, grad_out, grad_router, grad_mix, grad_gain_one, grad_gain_two = put_heads(
        ids, gather_pieces(heads_sum), w_qkv, gain_one, experts
    )
    return (
        output[None],
        input_grad[None],
        grad_qkv,
        grad_out,
        grad_fc1,
        grad_fc2,
        grad_router,
        grad_mix,
        grad_gain_one.reshape(held),
        grad_gain_two.reshape(held),
        grad_expert_in[None],
        grad_expert_out[None],
    )


def solution(mesh):
    return jax.shard_map(
        per_device,
        mesh=mesh,
        in_specs=(
            P("wide", "narrow", None),
            P("wide", None),
            P(("narrow", "wide"), None),
            P(),
            P(),
            P(),
            P(),
            P(),
            P(),
            P(),
            P(),
            P("wide", None, None),
            P("wide", None, None),
            P("wide", "narrow", None),
        ),
        out_specs=(
            P("wide", "narrow", None),
            P("wide", "narrow", None),
            P("wide", None),
            P("wide", None),
            P("wide", None),
            P("wide", None),
            P("wide", None),
            P("wide", None),
            P("wide"),
            P("wide"),
            P("wide", "narrow", None),
            P("wide", "narrow", None),
        ),
        check_vma=False,
    )
```

```python
import functools

import jax
import jax.numpy as jnp
from jax import lax
from jax.experimental import pallas as pl
from jax.experimental.pallas import tpu as pltpu
from jax.sharding import PartitionSpec as P

HEAD_DIM = 64
PAIR = 2 * HEAD_DIM
EPSILON = 1e-05
NEGATIVE_FILL = -1e30
VMEM_BYTES = 56 * 1024 * 1024
BF16 = jnp.bfloat16
F32 = jnp.float32


def normal_back(incoming, scaled, spread, gain):
    inner = incoming * gain
    return spread * (
        inner
        - jnp.mean(inner, axis=-1, keepdims=True)
        - scaled * jnp.mean(inner * scaled, axis=-1, keepdims=True)
    )


def dot(left, right, left_dim, right_dim):
    return lax.dot_general(
        left, right, (((left_dim,), (right_dim,)), ((), ())), preferred_element_type=F32
    )


def plain(left, right):
    return dot(left, right, 1, 0)


def across(left, right):
    return dot(left, right, 0, 0)


def beside(left, right):
    return dot(left, right, 1, 1)


def swap(values, axis, bit):
    size = lax.axis_size(axis)
    return lax.ppermute(values, axis, [(i, i ^ bit) for i in range(size)])


def x_bits():
    bits, bit = [], 2
    while bit < lax.axis_size("narrow"):
        bits.append(bit)
        bit *= 2
    return bits


def gather_pieces(values):
    pieces = [values]
    for bit in x_bits():
        pieces = pieces + [swap(piece, "narrow", bit) for piece in pieces]
    return pieces + [swap(piece, "narrow", 1) for piece in pieces]


def add_to_bf16(left, right):
    return (left.astype(F32) + right.astype(F32)).astype(BF16)


def scatter_addends(mine, other, rows):
    arrived = swap(other, "narrow", 1)
    bits = list(reversed(x_bits()))
    for bit in bits:
        half = mine.shape[0] // 2
        gone = add_to_bf16(mine[half:], arrived[half:])
        if bit == bits[-1]:
            return [mine, arrived, swap(gone, "narrow", bit)]
        mine, arrived = add_to_bf16(mine[:half], arrived[:half]), swap(gone, "narrow", bit)
    return [mine, arrived]


def natural_block(ids_ref, place, count):
    spots = count // 2
    return ids_ref[0] ^ (2 * (place % spots) + place // spots)


def natural_rows(ids_ref, place, count, rows):
    return pl.ds(pl.multiple_of(natural_block(ids_ref, place, count) * rows, rows), rows)


def params(steps=0):
    if steps:
        return pltpu.CompilerParams(
            vmem_limit_bytes=VMEM_BYTES, dimension_semantics=("arbitrary",) * steps
        )
    return pltpu.CompilerParams(vmem_limit_bytes=VMEM_BYTES)


def cost(flops, moved, curves=0):
    return pl.CostEstimate(flops=flops, bytes_accessed=moved, transcendentals=curves)


def in_vmem():
    return pl.BlockSpec(memory_space=pltpu.VMEM)


def in_smem():
    return pl.BlockSpec(memory_space=pltpu.SMEM)


def norm_kernel(tokens_ref, gain_ref, out_ref):
    scaled, _ = norm_rows(tokens_ref[...].astype(F32))
    out_ref[...] = (scaled * gain_ref[...].astype(F32)).astype(BF16)


def norm(tokens, gain):
    return pl.pallas_call(
        norm_kernel,
        out_shape=jax.ShapeDtypeStruct(tokens.shape, BF16),
        in_specs=[in_vmem()] * 2,
        out_specs=in_vmem(),
        compiler_params=params(),
        cost_estimate=cost(10 * tokens.size, 4 * tokens.size),
        name="norm",
    )(tokens, gain)


def heads_kernel(ids_ref, *refs):
    *piece_refs, weight_ref, out_ref = refs
    count, rows = len(piece_refs), piece_refs[0].shape[0]
    for place, piece_ref in enumerate(piece_refs):
        out_ref[natural_rows(ids_ref, place, count, rows), :] = plain(
            piece_ref[...], weight_ref[...]
        ).astype(BF16)


def to_heads(ids, pieces, w_qkv):
    count = len(pieces)
    rows, width = pieces[0].shape
    part = width // count
    whole = pl.BlockSpec((rows, width), lambda j, s: (0, 0))
    return pl.pallas_call(
        heads_kernel,
        grid_spec=pltpu.PrefetchScalarGridSpec(
            num_scalar_prefetch=1,
            grid=(3,),
            in_specs=[whole] * count
            + [pl.BlockSpec((width, part), lambda j, s: (0, j * count + s[0]))],
            out_specs=pl.BlockSpec((count * rows, part), lambda j, s: (0, j)),
        ),
        out_shape=jax.ShapeDtypeStruct((count * rows, 3 * part), BF16),
        compiler_params=params(1),
        cost_estimate=cost(6 * count * rows * width * part, 2 * width * (count * rows + 3 * part)),
        name="to_heads",
    )(ids, *pieces, w_qkv)


def from_heads_kernel(count, ids_ref, d_ref, *refs):
    *weight_refs, mine_ref, other_ref = refs
    rows = d_ref.shape[0] // count
    weight = jnp.concatenate([ref[...] for ref in weight_refs], axis=1)
    for place in range(count):
        result = beside(d_ref[natural_rows(ids_ref, place, count, rows), :], weight)
        into = mine_ref if place < count // 2 else other_ref
        at = (place % (count // 2)) * rows
        into[at : at + rows, :] = result.astype(BF16)


def from_heads(ids, d_qkv, w_qkv):
    count = lax.axis_size("narrow")
    length, width = d_qkv.shape[0], w_qkv.shape[0]
    part = width // count
    half = pl.BlockSpec((length // 2, width), lambda i, s: (0, 0))
    place = lambda j: (lambda i, s: (0, j * count + s[0]))
    return pl.pallas_call(
        functools.partial(from_heads_kernel, count),
        grid_spec=pltpu.PrefetchScalarGridSpec(
            num_scalar_prefetch=1,
            grid=(1,),
            in_specs=[pl.BlockSpec(d_qkv.shape, lambda i, s: (0, 0))]
            + [pl.BlockSpec((width, part), place(j)) for j in range(3)],
            out_specs=[half, half],
        ),
        out_shape=[jax.ShapeDtypeStruct((length // 2, width), BF16)] * 2,
        compiler_params=params(1),
        cost_estimate=cost(6 * length * width * part, 2 * length * width * 2),
        name="from_heads",
    )(ids, d_qkv, w_qkv, w_qkv, w_qkv)


def block_bias(seg_row_ref, seg_col_ref, block, rows):
    keys = (block + 1) * rows
    key_pos = lax.broadcasted_iota(jnp.int32, (keys, rows), 0)
    query_pos = lax.broadcasted_iota(jnp.int32, (keys, rows), 1) + block * rows
    same = seg_col_ref[0:keys, :] == seg_row_ref[:, block * rows : (block + 1) * rows]
    return jnp.where((key_pos <= query_pos) & same, 0.0, NEGATIVE_FILL)


def soft_columns(keys, query, bias):
    scores = beside(keys, query) * (HEAD_DIM**-0.5) + bias
    weights = jnp.exp(scores - jnp.max(scores, axis=0, keepdims=True))
    return weights * (1.0 / jnp.sum(weights, axis=0, keepdims=True))


def attend_kernel(count, seg_row_ref, seg_col_ref, qkv_ref, out_ref):
    width = out_ref.shape[1]
    rows = out_ref.shape[0] // count
    lane = lax.broadcasted_iota(jnp.int32, (rows, PAIR), 1)
    for block in range(count):
        span = slice(block * rows, (block + 1) * rows)
        seen = slice(0, (block + 1) * rows)
        bias = block_bias(seg_row_ref, seg_col_ref, block, rows)
        for pair in range(width // PAIR):
            columns = slice(pair * PAIR, (pair + 1) * PAIR)
            query = qkv_ref[span, columns]
            keys = qkv_ref[seen, width + pair * PAIR : width + (pair + 1) * PAIR]
            values = qkv_ref[seen, 2 * width + pair * PAIR : 2 * width + (pair + 1) * PAIR]
            halves = []
            for head in range(2):
                here = (lane // HEAD_DIM) == head
                probs = soft_columns(keys, jnp.where(here, query, 0), bias).astype(BF16)
                mixed = across(values, probs)
                halves.append(mixed[head * HEAD_DIM : (head + 1) * HEAD_DIM])
            out_ref[span, columns] = jnp.concatenate(halves, axis=0).T.astype(BF16)


def attend_back_kernel(count, seg_row_ref, seg_col_ref, qkv_ref, d_ref, out_ref, total_ref):
    width = d_ref.shape[1]
    rows = d_ref.shape[0] // count
    scale = HEAD_DIM**-0.5
    lane = lax.broadcasted_iota(jnp.int32, (rows, PAIR), 1)
    total_ref[...] = jnp.zeros_like(total_ref)
    for block in range(count):
        span = slice(block * rows, (block + 1) * rows)
        seen = slice(0, (block + 1) * rows)
        bias = block_bias(seg_row_ref, seg_col_ref, block, rows)
        for pair in range(width // PAIR):
            columns = slice(pair * PAIR, (pair + 1) * PAIR)
            key_columns = slice(width + pair * PAIR, width + (pair + 1) * PAIR)
            value_columns = slice(2 * width + pair * PAIR, 2 * width + (pair + 1) * PAIR)
            query = qkv_ref[span, columns]
            keys = qkv_ref[seen, key_columns]
            values = qkv_ref[seen, value_columns]
            incoming = d_ref[span, columns]
            halves = []
            for head in range(2):
                here = (lane // HEAD_DIM) == head
                own_query = jnp.where(here, query, 0)
                own_incoming = jnp.where(here, incoming, 0)
                probs = soft_columns(keys, own_query, bias)
                d_probs = beside(values, own_incoming)
                mean = jnp.sum(probs * d_probs, axis=0, keepdims=True)
                d_scores = (probs * (d_probs - mean)).astype(BF16)
                total_ref[seen, width + pair * PAIR : width + (pair + 1) * PAIR] += plain(
                    probs.astype(BF16), own_incoming
                )
                total_ref[seen, columns] += plain(d_scores, own_query)
                mixed = across(keys, d_scores)
                halves.append(mixed[head * HEAD_DIM : (head + 1) * HEAD_DIM])
            out_ref[span, columns] = (jnp.concatenate(halves, axis=0).T * scale).astype(BF16)
    out_ref[:, width : 2 * width] = (total_ref[:, :width] * scale).astype(BF16)
    out_ref[:, 2 * width :] = total_ref[:, width:].astype(BF16)


def attention_cost(length, width, matmuls):
    return cost(
        matmuls * length * length * width,
        length * width * 16,
        length * length * width // HEAD_DIM,
    )


def attend(seg_row, seg_col, qkv):
    length, width = qkv.shape[0], qkv.shape[1] // 3
    return pl.pallas_call(
        functools.partial(attend_kernel, lax.axis_size("narrow")),
        out_shape=jax.ShapeDtypeStruct((length, width), BF16),
        in_specs=[in_vmem()] * 3,
        out_specs=in_vmem(),
        compiler_params=params(),
        cost_estimate=attention_cost(length, width, 4),
        name="attend",
    )(seg_row, seg_col, qkv)


def attend_back(seg_row, seg_col, qkv, d_attended):
    length, width = d_attended.shape
    return pl.pallas_call(
        functools.partial(attend_back_kernel, lax.axis_size("narrow")),
        out_shape=jax.ShapeDtypeStruct(qkv.shape, BF16),
        in_specs=[in_vmem()] * 4,
        out_specs=in_vmem(),
        scratch_shapes=[pltpu.VMEM((length, 2 * width), F32)],
        compiler_params=params(),
        cost_estimate=attention_cost(length, width, 10),
        name="attend_back",
    )(seg_row, seg_col, qkv, d_attended)


def softmax_lanes(logits, here):
    weights = jnp.where(here, jnp.exp(logits - jnp.max(jnp.where(here, logits, NEGATIVE_FILL), axis=-1, keepdims=True)), 0.0)
    return weights * (1.0 / jnp.sum(weights, axis=-1, keepdims=True))


def norm_rows(values):
    centred = values - jnp.mean(values, axis=-1, keepdims=True)
    spread = lax.rsqrt(jnp.mean(centred * centred, axis=-1, keepdims=True) + EPSILON)
    return (centred * spread, spread)


def pick(gates, lane, index):
    return jnp.sum(jnp.where(lane == index, gates, 0.0), axis=-1, keepdims=True)


def middle_kernel(
    experts,
    capacity,
    parts_ref,
    w_out_ref,
    tokens_ref,
    d_ref,
    gain_ref,
    logit_ref,
    routes_ref,
    mid_ref,
    second_ref,
    d_dense_ref,
    slots_ref,
    d_slots_ref,
    to_slot_ref,
    gates_ref,
):
    count, rows, part = parts_ref.shape
    attended = jnp.concatenate([parts_ref[k] for k in range(count)], axis=1)
    mid = tokens_ref[...].astype(F32) + plain(attended, w_out_ref[...])
    mid_ref[...] = mid
    second = (norm_rows(mid)[0] * gain_ref[...].astype(F32)).astype(BF16)
    second_ref[...] = second
    logits = plain(second, logit_ref[...])
    lane = lax.broadcasted_iota(jnp.int32, logits.shape, 1)
    route_probs = softmax_lanes(logits, lane < experts)
    mixing = softmax_lanes(logits, (lane >= experts) & (lane < experts + 2))
    gates_ref[...] = route_probs + mixing
    routes = routes_ref[...]
    chosen = lane == routes
    gate = jnp.sum(jnp.where(chosen, route_probs, 0.0), axis=-1, keepdims=True)
    d_output = d_ref[...].astype(F32)
    d_dense_ref[...] = (d_output * pick(mixing, lane, experts)).astype(BF16)
    d_expert = (d_output * pick(mixing, lane, experts + 1) * gate).astype(BF16)
    before = (
        lax.broadcasted_iota(jnp.int32, (rows, rows), 1)
        < lax.broadcasted_iota(jnp.int32, (rows, rows), 0)
    ).astype(F32).astype(BF16)
    earlier = plain(before, chosen.astype(F32).astype(BF16))
    position = jnp.sum(jnp.where(chosen, earlier, 0.0), axis=-1, keepdims=True)
    slot = routes * capacity + position.astype(jnp.int32)
    slots = experts * capacity
    to_slot = (
        (lax.broadcasted_iota(jnp.int32, (rows, slots), 1) == slot).astype(F32).astype(BF16)
    )
    to_slot_ref[...] = to_slot
    slots_ref[...] = across(to_slot, second).astype(BF16)
    d_slots_ref[...] = across(to_slot, d_expert).astype(BF16)


def middle(parts, w_out, tokens, d_output, gain, logit_weight, routes, experts, capacity):
    rows, width = tokens.shape
    slots = experts * capacity
    lanes = logit_weight.shape[1]
    return pl.pallas_call(
        functools.partial(middle_kernel, experts, capacity),
        out_shape=[
            jax.ShapeDtypeStruct((rows, width), F32),
            jax.ShapeDtypeStruct((rows, width), BF16),
            jax.ShapeDtypeStruct((rows, width), BF16),
            jax.ShapeDtypeStruct((slots, width), BF16),
            jax.ShapeDtypeStruct((slots, width), BF16),
            jax.ShapeDtypeStruct((rows, slots), BF16),
            jax.ShapeDtypeStruct((rows, lanes), F32),
        ],
        in_specs=[in_vmem()] * 7,
        out_specs=[in_vmem()] * 7,
        compiler_params=params(),
        cost_estimate=cost(2 * rows * width * (width + 2 * slots), 2 * width * (width + 8 * rows)),
        name="middle",
    )(parts, w_out, tokens, d_output, gain, logit_weight, routes)


def merge_kernel(
    experts,
    results,
    back_ref,
    d_back_ref,
    to_slot_ref,
    gates_ref,
    routes_ref,
    mid_ref,
    second_ref,
    d_ref,
    gain_ref,
    logit_ref,
    w_out_ref,
    *refs,
):
    sums, outs = refs[: 2 * results], refs[2 * results :]
    output_ref, d_mid_ref, d_attn_ref, d_attended_ref, small_ref = outs
    to_slot = to_slot_ref[...]
    expert_result = plain(to_slot, back_ref[...])
    d_second = plain(to_slot, d_back_ref[...])
    dense_result = sums[0][...].astype(F32)
    for ref in sums[1:results]:
        dense_result = dense_result + ref[...].astype(F32)
    for ref in sums[results:]:
        d_second = d_second + ref[...].astype(F32)
    gates = gates_ref[...]
    lane = lax.broadcasted_iota(jnp.int32, gates.shape, 1)
    chosen = lane == routes_ref[...]
    gate = pick(gates, lane, routes_ref[...])
    mix_dense, mix_expert = pick(gates, lane, experts), pick(gates, lane, experts + 1)
    mid = mid_ref[...]
    d_output = d_ref[...].astype(F32)
    output_ref[...] = (
        mid + mix_dense * dense_result + mix_expert * gate * expert_result
    ).astype(BF16)
    on_dense = jnp.sum(d_output * dense_result, axis=-1, keepdims=True)
    on_expert = jnp.sum(d_output * expert_result, axis=-1, keepdims=True)
    mean = mix_dense * on_dense + mix_expert * (gate * on_expert)
    d_mix = gates * (jnp.where(lane == experts, on_dense, gate * on_expert) - mean)
    d_route = gates * (chosen.astype(F32) - gate) * (mix_expert * on_expert)
    d_logits = jnp.where(
        lane < experts, d_route, jnp.where(lane < experts + 2, d_mix, 0.0)
    ).astype(BF16)
    d_second = d_second + beside(d_logits, logit_ref[...])
    scaled, spread = norm_rows(mid)
    d_gain = jnp.sum(d_second * scaled, axis=0, keepdims=True)
    d_mid = d_output + normal_back(d_second, scaled, spread, gain_ref[...].astype(F32))
    d_mid_ref[...] = d_mid
    d_attn = d_mid.astype(BF16)
    d_attended = beside(d_attn, w_out_ref[...]).astype(BF16)
    count, rows, part = d_attn_ref.shape
    for block in range(count):
        d_attn_ref[block] = d_attn[:, block * part : (block + 1) * part]
        d_attended_ref[block] = d_attended[:, block * part : (block + 1) * part]
    small = across(second_ref[...], d_logits)
    column = jnp.broadcast_to(d_gain, (small.shape[1], small.shape[0])).T
    small_lane = lax.broadcasted_iota(jnp.int32, small.shape, 1)
    small_ref[...] = jnp.where(small_lane == experts + 2, column, small).astype(BF16)


def merge(back, d_back, to_slot, gates, routes, mid, second, d_output, gain, logit_weight, w_out,
          dense_sums, d_second_sums, experts, count):
    rows, width = mid.shape
    part = width // count
    slots = to_slot.shape[1]
    lanes = logit_weight.shape[1]
    whole = lambda v: pl.BlockSpec(v.shape, lambda i: (0,) * v.ndim)
    top = pl.BlockSpec((rows, width), lambda i: (0, 0))
    blocks = pl.BlockSpec((count, rows, part), lambda i: (0, 0, 0))
    given = (back, d_back, to_slot, gates, routes, mid, second, d_output, gain, logit_weight, w_out)
    return pl.pallas_call(
        functools.partial(merge_kernel, experts, len(dense_sums)),
        grid=(1,),
        out_shape=[
            jax.ShapeDtypeStruct((rows, width), BF16),
            jax.ShapeDtypeStruct((rows, width), F32),
            jax.ShapeDtypeStruct((count, rows, part), BF16),
            jax.ShapeDtypeStruct((count, rows, part), BF16),
            jax.ShapeDtypeStruct((width, lanes), BF16),
        ],
        in_specs=[whole(v) for v in given] + [top] * (2 * len(dense_sums)),
        out_specs=[top, top, blocks, blocks, pl.BlockSpec((width, lanes), lambda i: (0, 0))],
        compiler_params=params(1),
        cost_estimate=cost(2 * rows * width * (width + 2 * slots), 2 * width * (width + 16 * rows)),
        name="merge",
    )(*given, *dense_sums, *d_second_sums)


def finish_kernel(tokens_ref, gain_ref, d_mid_ref, *refs):
    *sum_refs, out_ref = refs
    incoming = sum_refs[0][...].astype(F32)
    for ref in sum_refs[1:]:
        incoming = incoming + ref[...].astype(F32)
    scaled, spread = norm_rows(tokens_ref[...].astype(F32))
    out_ref[...] = d_mid_ref[...] + normal_back(
        incoming, scaled, spread, gain_ref[...].astype(F32)
    )


def finish(tokens, gain, d_mid, sums):
    rows, width = tokens.shape
    top = pl.BlockSpec((rows, width), lambda i: (0, 0))
    return pl.pallas_call(
        finish_kernel,
        grid=(1,),
        out_shape=jax.ShapeDtypeStruct((rows, width), F32),
        in_specs=[top, pl.BlockSpec((1, width), lambda i: (0, 0)), top] + [top] * len(sums),
        out_specs=top,
        compiler_params=params(1),
        cost_estimate=cost(20 * rows * width, 20 * rows * width),
        name="finish",
    )(tokens, gain, d_mid, *sums)


def whole_rows(refs):
    return jnp.concatenate([ref[...] for ref in refs], axis=0)


def whole_columns(refs):
    return jnp.concatenate([ref[...] for ref in refs], axis=1)


def row_chunks(refs, size):
    chunks, at = [], 0
    for ref in refs:
        for start in range(0, ref.shape[0], size):
            chunks.append((ref, start, at + start))
        at += ref.shape[0]
    return chunks


CHUNK = 256


def write_halves(total_ref, mine_ref, other_ref):
    @pl.when(pl.program_id(0) == pl.num_programs(0) - 1)
    def _():
        half = mine_ref.shape[0]
        mine_ref[...] = total_ref[:half, :].astype(BF16)
        other_ref[...] = total_ref[half:, :].astype(BF16)


def clear_first(total_ref):
    @pl.when(pl.program_id(0) == 0)
    def _():
        total_ref[...] = jnp.zeros_like(total_ref)


def forward_kernel(pieces, slices, ids_ref, *refs):
    piece_refs, refs = refs[:pieces], refs[pieces:]
    in_refs, out_refs, refs = refs[:slices], refs[slices : 2 * slices], refs[2 * slices :]
    hidden_ref, slope_ref, mine_ref, other_ref, total_ref = refs
    clear_first(total_ref)
    weight_in, weight_out = whole_columns(in_refs), whole_rows(out_refs)
    chunks = row_chunks(piece_refs, CHUNK)
    first_dot = lambda c: plain(c[0][c[1] : c[1] + CHUNK, :], weight_in)
    pre = first_dot(chunks[0])
    for index, (_, _, at) in enumerate(chunks):
        later = first_dot(chunks[index + 1]) if index + 1 < len(chunks) else None
        square = pre * pre
        curve = jnp.tanh(pre * (0.7978845608 + (0.7978845608 * 0.044715) * square))
        half = 0.5 + 0.5 * curve
        hidden = (pre * half).astype(BF16)
        slope = half + (0.5 * pre) * (1.0 - curve * curve) * (
            0.7978845608 + (3.0 * 0.7978845608 * 0.044715) * square
        )
        hidden_ref[at : at + CHUNK, :] = hidden
        slope_ref[at : at + CHUNK, :] = slope.astype(BF16)
        total_ref[at : at + CHUNK, :] += plain(hidden, weight_out)
        pre = later
    write_halves(total_ref, mine_ref, other_ref)


def backward_kernel(pieces, slices, ids_ref, *refs):
    piece_refs, refs = refs[:pieces], refs[pieces:]
    in_refs, out_refs, refs = refs[:slices], refs[slices : 2 * slices], refs[2 * slices :]
    slope_ref, d_pre_ref, mine_ref, other_ref, total_ref = refs
    clear_first(total_ref)
    weight_in, weight_out = whole_columns(in_refs), whole_rows(out_refs)
    chunks = row_chunks(piece_refs, CHUNK)
    first_dot = lambda c: beside(c[0][c[1] : c[1] + CHUNK, :], weight_out)
    d_hidden = first_dot(chunks[0])
    for index, (_, _, at) in enumerate(chunks):
        later = first_dot(chunks[index + 1]) if index + 1 < len(chunks) else None
        d_pre = (d_hidden * slope_ref[at : at + CHUNK, :].astype(F32)).astype(BF16)
        d_pre_ref[at : at + CHUNK, :] = d_pre
        total_ref[at : at + CHUNK, :] += beside(d_pre, weight_in)
        d_hidden = later
    write_halves(total_ref, mine_ref, other_ref)


def feed(kernel, name, ids, pieces, weight_in, weight_out, units, places, block, slope=None):
    width = pieces[0].shape[1]
    count = sum(piece.shape[0] for piece in pieces)
    size = block // len(places)
    unit_spec = pl.BlockSpec((count, block), lambda f, s: (0, f))
    half_spec = pl.BlockSpec((count // 2, width), lambda f, s: (0, 0))
    in_places = [(lambda f, s, p=p: (0, p(f, s))) for p in places]
    out_places = [(lambda f, s, p=p: (p(f, s), 0)) for p in places]
    in_specs = (
        [pl.BlockSpec(piece.shape, lambda f, s: (0, 0)) for piece in pieces]
        + [pl.BlockSpec((width, size), p) for p in in_places]
        + [pl.BlockSpec((size, width), p) for p in out_places]
    )
    given = [*pieces] + [weight_in] * len(places) + [weight_out] * len(places)
    if slope is not None:
        in_specs.append(unit_spec)
        given.append(slope)
    unit_outs = 2 if slope is None else 1
    return pl.pallas_call(
        functools.partial(kernel, len(pieces), len(places)),
        grid_spec=pltpu.PrefetchScalarGridSpec(
            num_scalar_prefetch=1,
            grid=(units // block,),
            in_specs=in_specs,
            out_specs=[unit_spec] * unit_outs + [half_spec] * 2,
            scratch_shapes=[pltpu.VMEM((count, width), F32)],
        ),
        out_shape=[jax.ShapeDtypeStruct((count, units), BF16)] * unit_outs
        + [jax.ShapeDtypeStruct((count // 2, width), BF16)] * 2,
        compiler_params=params(1),
        cost_estimate=cost(
            4 * count * width * units,
            2 * (2 * count * width + 2 * width * units + 2 * count * units),
            count * units,
        ),
        name=name,
    )(ids, *given)


def grad_kernel(lefts, rights, ids_ref, *refs):
    left = whole_rows(refs[:lefts])
    right = whole_rows(refs[lefts : lefts + rights])
    total = across(left, right)
    for ref in refs[lefts + rights : -1]:
        total = total + ref[...].astype(F32)
    refs[-1][...] = total.astype(refs[-1].dtype)


def grad(name, ids, lefts, rights, rows, steps, left_place, columns=None, right_place=None,
         added=None, added_place=None, out=None, out_place=None, dtype=BF16):
    depth = sum(v.shape[0] for v in lefts)
    columns = columns or rights[0].shape[1]
    right_place = right_place or (lambda i, s: 0)
    out_place = out_place or (lambda i, s: (i, 0))
    out = out or (rows * steps, columns)
    in_specs = [
        pl.BlockSpec((v.shape[0], rows), lambda i, s: (0, left_place(i, s))) for v in lefts
    ] + [pl.BlockSpec((v.shape[0], columns), lambda i, s: (0, right_place(i, s))) for v in rights]
    given = [*lefts, *rights]
    if added is not None:
        in_specs.append(pl.BlockSpec((rows, columns), added_place or out_place))
        given.append(added)
    return pl.pallas_call(
        functools.partial(grad_kernel, len(lefts), len(rights)),
        grid_spec=pltpu.PrefetchScalarGridSpec(
            num_scalar_prefetch=1,
            grid=(steps,),
            in_specs=in_specs,
            out_specs=pl.BlockSpec((rows, columns), out_place),
        ),
        out_shape=jax.ShapeDtypeStruct(out, dtype),
        compiler_params=params(1),
        cost_estimate=cost(
            2 * depth * rows * steps * columns,
            2 * (depth * (rows * steps + columns) + 2 * rows * steps * columns),
        ),
        name=name,
    )(ids, *given)


def feed_grads_kernel(pieces, ids_ref, hidden_ref, d_pre_ref, *refs):
    row_refs, d_refs, (keep_ref, gone_ref) = refs[:pieces], refs[pieces:-2], refs[-2:]
    part = d_pre_ref.shape[1]
    half = keep_ref.shape[0]
    swapped = (ids_ref[3] & 1) == 1

    def put(total, columns):
        total = total.astype(BF16)
        keep_ref[:, columns] = jnp.where(swapped, total[half:], total[:half])
        gone_ref[:, columns] = jnp.where(swapped, total[:half], total[half:])

    put(across(whole_rows(row_refs), d_pre_ref[...]), slice(0, part))
    put(across(hidden_ref[...], whole_rows(d_refs)), slice(part, part + keep_ref.shape[1] - part))


def feed_grads(ids, rows, d_rows, hidden, d_pre):
    count, width = rows[0].shape
    length, part = d_pre.shape
    steps = lax.axis_size("wide") // 2
    fixed = lambda v: pl.BlockSpec(v.shape, lambda i, s: (0, 0))
    out = jax.ShapeDtypeStruct((width // 2, part + width), BF16)
    out_spec = pl.BlockSpec((width // steps // 2, part + width), lambda i, s: (i, 0))
    return pl.pallas_call(
        functools.partial(feed_grads_kernel, len(rows)),
        grid_spec=pltpu.PrefetchScalarGridSpec(
            num_scalar_prefetch=1,
            grid=(steps,),
            in_specs=[pl.BlockSpec((length, part // steps), lambda i, s: (0, i)), fixed(d_pre)]
            + [pl.BlockSpec((count, width // steps), lambda i, s: (0, i))] * len(rows)
            + [fixed(v) for v in d_rows],
            out_specs=[out_spec, out_spec],
        ),
        out_shape=[out, out],
        compiler_params=params(1),
        cost_estimate=cost(4 * length * width * part, 2 * (4 * length * width + 2 * width * part)),
        name="feed_grads",
    )(ids, hidden, d_pre, *rows, *d_rows)


def heads_grad_kernel(count, ids_ref, *refs):
    piece_refs, (d_ref, out_sum_ref, small_ref, out_ref) = refs[:count], refs[count:]
    rows = piece_refs[0].shape[0]
    right = jnp.concatenate(
        [d_ref[natural_rows(ids_ref, place, count, rows), :] for place in range(count)], axis=0
    )
    triple, part = right.shape[1], out_sum_ref.shape[1]
    out_ref[:, :triple] = across(whole_rows(piece_refs), right).astype(BF16)
    out_ref[:, triple : triple + part] = out_sum_ref[...]
    out_ref[:, triple + part :] = small_ref[...]


def heads_grad(ids, pieces, d_qkv, out_sum, small):
    rows, width = pieces[0].shape
    length, triple = d_qkv.shape
    part, lanes = out_sum.shape[1], small.shape[1]
    block = 256
    return pl.pallas_call(
        functools.partial(heads_grad_kernel, len(pieces)),
        grid_spec=pltpu.PrefetchScalarGridSpec(
            num_scalar_prefetch=1,
            grid=(width // block,),
            in_specs=[pl.BlockSpec((rows, block), lambda i, s: (0, i))] * len(pieces)
            + [
                pl.BlockSpec(d_qkv.shape, lambda i, s: (0, 0)),
                pl.BlockSpec((block, part), lambda i, s: (i, 0)),
                pl.BlockSpec((block, lanes), lambda i, s: (i, 0)),
            ],
            out_specs=pl.BlockSpec((block, triple + part + lanes), lambda i, s: (i, 0)),
        ),
        out_shape=jax.ShapeDtypeStruct((width, triple + part + lanes), BF16),
        compiler_params=params(1),
        cost_estimate=cost(2 * length * width * triple, 4 * length * width),
        name="heads_grad",
    )(ids, *pieces, d_qkv, out_sum, small)


def out_grad_kernel(ids_ref, attended_ref, d_ref, mine_ref, other_ref):
    count, _, part = d_ref.shape
    spots = count // 2
    for place in range(count):
        total = across(attended_ref[0], d_ref[natural_block(ids_ref, place, count)])
        into = mine_ref if place < spots else other_ref
        at = (place % spots) * part
        into[:, at : at + part] = total.astype(BF16)


def out_grad(ids, attended, d_attn):
    count, rows, part = attended.shape
    out = jax.ShapeDtypeStruct((count * part, count * part // 2), BF16)
    out_spec = pl.BlockSpec((part, count * part // 2), lambda i, s: (i, 0))
    return pl.pallas_call(
        out_grad_kernel,
        grid_spec=pltpu.PrefetchScalarGridSpec(
            num_scalar_prefetch=1,
            grid=(count,),
            in_specs=[
                pl.BlockSpec((1, rows, part), lambda i, s: (i, 0, 0)),
                pl.BlockSpec(d_attn.shape, lambda i, s: (0, 0, 0)),
            ],
            out_specs=[out_spec, out_spec],
        ),
        out_shape=[out, out],
        compiler_params=params(1),
        cost_estimate=cost(2 * rows * (part * count) ** 2, 8 * (part * count) ** 2),
        name="out_grad",
    )(ids, attended, d_attn)


def scatter_columns(mine, other, columns):
    total = add_to_bf16(mine, swap(other, "narrow", 1))
    for bit in reversed(x_bits()):
        half = total.shape[1] // 2
        total = add_to_bf16(total[:, :half], swap(total[:, half:], "narrow", bit))
    return total


def put_feed_kernel(count, all_ref, first_out_ref, second_out_ref):
    held, width = all_ref.shape[1], second_out_ref.shape[1]
    part = all_ref.shape[2] - width
    for n in range(count):
        for w in range(part // held):
            at = (w * count + n) * held
            first_out_ref[:, at : at + held] = all_ref[n][:, w * held : (w + 1) * held].astype(F32)
        second_out_ref[n * held : (n + 1) * held, :] = all_ref[n][:, part:].astype(F32)


def put_feed(feed_all, width):
    count, held, both = feed_all.shape
    part = both - width
    return pl.pallas_call(
        functools.partial(put_feed_kernel, count),
        out_shape=[
            jax.ShapeDtypeStruct((held, count * part), F32),
            jax.ShapeDtypeStruct((count * held, width), F32),
        ],
        in_specs=[in_vmem()],
        out_specs=[in_vmem()] * 2,
        compiler_params=params(),
        cost_estimate=cost(0, 6 * count * held * both),
        name="put_feed",
    )(feed_all)


def put_heads_kernel(count, experts, ids_ref, *refs):
    piece_refs, refs = refs[:count], refs[count:]
    w_ref, gain_ref, grad_qkv_ref, grad_out_ref, router_ref, mix_ref, one_ref, two_ref = refs
    width = w_ref.shape[1] // 3
    part = width // count
    small = None
    for place in range(count):
        n = natural_block(ids_ref, place, count)
        for j in range(3):
            at = pl.multiple_of(j * width + n * part, part)
            grad_qkv_ref[:, pl.ds(at, part)] = piece_refs[place][
                :, j * part : (j + 1) * part
            ].astype(F32)
        at = pl.multiple_of(n * part, part)
        grad_out_ref[:, pl.ds(at, part)] = piece_refs[place][:, 3 * part : 4 * part].astype(F32)
        its = piece_refs[place][:, 4 * part :].astype(F32)
        small = its if small is None else small + its
    turned = small.T
    router_ref[...] = turned[:experts, :]
    mix_ref[...] = turned[experts : experts + 2, :]
    two_ref[...] = turned[experts + 2 : experts + 3, :]
    weighed = jnp.sum(w_ref[...].astype(F32) * grad_qkv_ref[...], axis=1, keepdims=True)
    weighed = jnp.broadcast_to(weighed, small.shape).T[0:1, :]
    one_ref[...] = weighed / gain_ref[0].astype(F32)


def put_heads(ids, pieces, w_qkv, gain, experts):
    count = len(pieces)
    held = pieces[0].shape[0]
    width = w_qkv.shape[0]
    fixed = lambda shape: pl.BlockSpec(shape, lambda i, s: (0,) * len(shape))
    outs = [(held, 3 * width), (held, width), (experts, held), (2, held), (1, held), (1, held)]
    return pl.pallas_call(
        functools.partial(put_heads_kernel, count, experts),
        grid_spec=pltpu.PrefetchScalarGridSpec(
            num_scalar_prefetch=1,
            grid=(1,),
            in_specs=[fixed(v.shape) for v in pieces]
            + [
                pl.BlockSpec((held, 3 * width), lambda i, s: (s[3], 0)),
                pl.BlockSpec((1, 1, held), lambda i, s: (s[3], 0, 0)),
            ],
            out_specs=[fixed(shape) for shape in outs],
        ),
        out_shape=[jax.ShapeDtypeStruct(shape, F32) for shape in outs],
        compiler_params=params(1),
        cost_estimate=cost(2 * held * 3 * width, 20 * held * width),
        name="put_heads",
    )(ids, *pieces, w_qkv, gain.reshape(width // held, 1, held))


def fill_kernel(ids_ref, half_ref, whole_ref, out_ref):
    out_ref[...] = half_ref[...].astype(F32)


def fill_other(ids, half, whole):
    rows, columns = half.shape
    spots = lax.axis_size("narrow") // 2
    quarter = columns // spots
    return pl.pallas_call(
        fill_kernel,
        grid_spec=pltpu.PrefetchScalarGridSpec(
            num_scalar_prefetch=1,
            grid=(spots,),
            in_specs=[
                pl.BlockSpec((rows, quarter), lambda i, s: (0, i)),
                pl.BlockSpec(memory_space=pl.ANY),
            ],
            out_specs=pl.BlockSpec((rows, quarter), lambda i, s: (0, 2 * i + 1 - s[1])),
        ),
        out_shape=jax.ShapeDtypeStruct(whole.shape, F32),
        input_output_aliases={2: 0},
        compiler_params=params(1),
        cost_estimate=cost(0, 6 * rows * columns),
        name="fill_other",
    )(ids, half, whole)


def wide_sum(values):
    return lax.psum_scatter(values, "wide", scatter_dimension=0, tiled=True)


def wide_sum_at_once(values, after):
    wide = lax.axis_size("wide")
    blocks = values.reshape(wide, values.shape[0] // wide, values.shape[1])
    arrived = lax.all_to_all(blocks, "wide", split_axis=0, concat_axis=0, tiled=True)
    return jnp.sum(tied(arrived, *after).astype(F32), axis=0).astype(BF16)


def narrow_all(values):
    return lax.all_gather(values, "narrow", axis=0, tiled=False)


def tied(value, *others):
    return lax.optimization_barrier((value, *others))[0]


def out_leaves(ids, d_rows, hidden):
    block = min(512, hidden.shape[1] // 2)
    per = hidden.shape[1] // 2 // block
    return grad("out_gone", ids, [hidden], d_rows, block, per, lambda i, s: (1 - s[2]) * per + i)


def in_leaves(ids, rows, d_pre):
    part = rows[0].shape[1] // 4
    return grad("in_gone", ids, rows, [d_pre], part, 2, lambda i, s: 2 * (1 - s[2]) + i)


def expert_grads(ids, rows, d_rows, hidden, d_pre, own, out_came, in_came, later):
    narrow = lax.axis_size("narrow")
    spots = narrow // 2
    width, shared = rows[0].shape[1], hidden.shape[1]
    quarter = shared // spots
    part = width // narrow
    if spots == 2:
        block = min(512, quarter)
        per = quarter // block
        hidden = tied(hidden, later)
        grad_out = grad("out_kept", ids, [hidden], d_rows, block, per,
                        lambda i, s: s[2] * per + i, added=out_came, dtype=F32)
        in_other = grad("in_other", ids, rows, [d_pre], part, 1,
                        lambda i, s: 2 * s[2] + 1 - s[1], added=in_came,
                        added_place=lambda i, s: (1 - s[1], 0))
        in_arrived = swap(in_other, "narrow", 1)
        in_kept = grad("in_kept", ids, rows, [d_pre], part, spots,
                       lambda i, s: 2 * s[2] + s[1], columns=quarter,
                       right_place=lambda i, s: i, added=in_came,
                       added_place=lambda i, s: (s[1], i),
                       out=(part, 2 * shared), out_place=lambda i, s: (0, 2 * i + s[1]),
                       dtype=F32)
        return fill_other(ids, in_arrived, in_kept), grad_out
    groups = [[2 * x + c for x in range(spots)] for c in range(2)]
    all_rows = jnp.concatenate(rows, axis=0)
    all_d_rows = jnp.concatenate(d_rows, axis=0)
    over_x = lambda v: lax.psum_scatter(
        v.astype(BF16), "narrow", scatter_dimension=0, axis_index_groups=groups, tiled=True
    )
    grad_out = over_x(across(hidden, all_d_rows)).astype(F32)
    in_sum = over_x(across(all_rows, d_pre)).reshape(2, part, shared)
    core = own & 1
    kept = lax.dynamic_index_in_dim(in_sum, core, 0, keepdims=False).astype(F32)
    gone = lax.dynamic_index_in_dim(in_sum, 1 - core, 0, keepdims=False)
    came = swap(gone, "narrow", 1).astype(F32)
    even = jnp.where(core == 0, kept, came).reshape(part, spots, 1, quarter)
    odd = jnp.where(core == 0, came, kept).reshape(part, spots, 1, quarter)
    grad_in = jnp.concatenate([even, odd], axis=2).reshape(part, 2 * shared)
    return grad_in, grad_out


def per_device(
    tokens,
    segments,
    routes,
    w_qkv,
    w_out,
    w_fc1,
    w_fc2,
    router,
    mix_weight,
    gain_one,
    gain_two,
    expert_in,
    expert_out,
    cotangent,
):
    rows, width = tokens.shape[1:]
    length = segments.shape[1]
    experts = router.shape[1]
    capacity = 2 * rows // experts
    narrow, wide = lax.axis_size("narrow"), lax.axis_size("wide")
    own = lax.axis_index("narrow")
    units = w_fc1.shape[1]
    part = width // narrow
    ids = jnp.stack([own, own & 1, own >> 1, lax.axis_index("wide")]).astype(jnp.int32)
    seg_row, seg_col = segments.reshape(1, length), segments.reshape(length, 1)
    own_tokens, d_output = tokens[0], cotangent[0]
    gain_row_one, gain_row_two = gain_one.reshape(1, width), gain_two.reshape(1, width)
    lanes = -(-(experts + 3) // 128) * 128
    logit_weight = jnp.concatenate(
        [router, mix_weight, jnp.zeros((width, lanes - experts - 2), BF16)], axis=1
    )

    first = norm(own_tokens, gain_row_one)
    first_pieces = gather_pieces(first)
    qkv = to_heads(ids, first_pieces, w_qkv)
    attended_part = attend(seg_row, seg_col, qkv)
    attended = lax.all_to_all(
        attended_part.reshape(narrow, rows, part), "narrow", split_axis=0, concat_axis=0, tiled=True
    )
    mid, second, d_dense, slots, d_slots, to_slot, gates = middle(
        attended, w_out, own_tokens, d_output, gain_row_two, logit_weight, routes, experts, capacity
    )

    def to_experts(values):
        values = values.reshape(experts, capacity, width)
        arrived = lax.all_to_all(values, "wide", split_axis=0, concat_axis=0, tiled=True)
        return arrived.reshape(experts * capacity, width)

    def to_tokens(both):
        both = both.reshape(experts, capacity, width)
        back = lax.all_to_all(both, "wide", split_axis=0, concat_axis=0, tiled=True)
        return back.reshape(experts * capacity, width)

    expert_rows = to_experts(slots)

    slot = units // (wide * narrow)
    dense_units = units // narrow
    dense_block = min(512, dense_units)
    if slot % 128 == 0:
        slices = dense_block // slot
        dense_places = [
            (lambda f, s, i=i: (f * slices + i) * narrow + s[0]) for i in range(slices)
        ]
        fc1_part, fc2_part = w_fc1, w_fc2
    else:
        dense_places = [lambda f, s: f]
        fc1_part = lax.dynamic_index_in_dim(
            w_fc1.reshape(width, wide, narrow, slot), own, 2, keepdims=False
        ).reshape(width, dense_units)
        fc2_part = lax.dynamic_index_in_dim(
            w_fc2.reshape(wide, narrow, slot, width), own, 1, keepdims=False
        ).reshape(dense_units, width)
    second_pieces = gather_pieces(second)
    d_dense_pieces = gather_pieces(d_dense)
    dense_hidden, dense_slope, dense_mine, dense_other = feed(
        forward_kernel, "dense_forward", ids, second_pieces, fc1_part, fc2_part,
        dense_units, dense_places, dense_block,
    )
    expert_rows = tied(expert_rows, dense_hidden)
    expert_d_rows = to_experts(tied(d_slots, expert_rows))
    expert_rows = [expert_rows, swap(expert_rows, "narrow", 1)]
    expert_d_rows = [expert_d_rows, swap(expert_d_rows, "narrow", 1)]
    dense_sums = scatter_addends(dense_mine, dense_other, rows)
    d_dense_pre, d_second_mine, d_second_other = feed(
        backward_kernel, "dense_backward", ids, d_dense_pieces, fc1_part, fc2_part,
        dense_units, dense_places, dense_block, dense_slope,
    )
    d_second_sums = scatter_addends(d_second_mine, d_second_other, rows)

    quarter = units // narrow
    expert_block = min(512, quarter)
    per_quarter = quarter // expert_block
    expert_places = [
        lambda f, s: (2 * (f // per_quarter) + s[1]) * per_quarter + f % per_quarter
    ]
    expert_rows = [tied(expert_rows[0], d_second_mine), expert_rows[1]]
    expert_hidden, expert_slope, produced_mine, produced_other = feed(
        forward_kernel, "expert_forward", ids, expert_rows, expert_in[0], expert_out[0],
        units // 2, expert_places, expert_block,
    )
    produced = add_to_bf16(produced_mine, swap(produced_other, "narrow", 1))
    back = to_tokens(produced)
    out_gone = out_leaves(ids, expert_d_rows, expert_hidden) if narrow == 4 else produced
    d_expert_pre, d_sent_mine, d_sent_other = feed(
        backward_kernel, "expert_backward", ids, expert_d_rows, expert_in[0], expert_out[0],
        units // 2, expert_places, expert_block, tied(expert_slope, out_gone, produced, dense_sums[-1], d_second_sums[-1]),
    )
    d_back = to_tokens(add_to_bf16(d_sent_mine, swap(d_sent_other, "narrow", 1)))
    dense_hidden = tied(dense_hidden, back, d_expert_pre)
    if slot % 128 == 0:
        feed_keep, feed_gone = feed_grads(
            ids, second_pieces, d_dense_pieces, dense_hidden, d_dense_pre
        )
    else:
        fc1_sum = wide_sum(
            grad("fc1_grad", ids, second_pieces, [d_dense_pre], 256, width // 256, lambda i, s: i)
        )
        fc2_sum = wide_sum(
            grad("fc2_grad", ids, [dense_hidden], d_dense_pieces, 256, dense_units // 256,
                 lambda i, s: i)
        )

    in_gone = in_leaves(ids, expert_rows, d_expert_pre) if narrow == 4 else d_back
    out_came, in_came = swap(out_gone, "narrow", 2), swap(in_gone, "narrow", 2)

    output, d_mid, d_attn, d_attended, small = merge(
        back, d_back, tied(to_slot, in_gone, out_came), gates, routes, mid, second, d_output, gain_row_two, logit_weight,
        w_out, dense_sums, d_second_sums, experts, narrow,
    )
    d_attended_part = lax.all_to_all(
        d_attended, "narrow", split_axis=0, concat_axis=0, tiled=True
    ).reshape(length, part)
    out_mine, out_other = out_grad(ids, attended, d_attn)
    out_sum = scatter_columns(out_mine, out_other, part)
    if slot % 128 == 0:
        feed_sum = lax.psum_scatter(
            add_to_bf16(tied(feed_keep, d_attended), swap(feed_gone, "wide", 1)),
            "wide",
            scatter_dimension=0,
            axis_index_groups=[[2 * z + y for z in range(wide // 2)] for y in range(2)],
            tiled=True,
        )
    d_qkv = attend_back(seg_row, seg_col, tied(qkv, out_mine), d_attended_part)
    d_first_mine, d_first_other = from_heads(ids, d_qkv, w_qkv)
    d_first_sums = scatter_addends(d_first_mine, d_first_other, rows)
    heads_total = heads_grad(ids, first_pieces, tied(d_qkv, in_came), out_sum, small)
    input_grad = finish(own_tokens, gain_row_one, d_mid, d_first_sums)
    grad_expert_in, grad_expert_out = expert_grads(
        ids, expert_rows, expert_d_rows, expert_hidden, d_expert_pre, own, out_came, in_came, d_qkv
    )
    heads_sum = wide_sum_at_once(heads_total, (grad_expert_out,))

    held = width // wide
    if slot % 128 == 0:
        grad_fc1, grad_fc2 = put_feed(narrow_all(feed_sum), width)
    else:
        fc1_all, fc2_all = narrow_all(fc1_sum), narrow_all(fc2_sum)
        grad_fc1 = (
            fc1_all.reshape(narrow, held, wide, slot).transpose(1, 2, 0, 3).reshape(held, units)
        ).astype(F32)
        grad_fc2 = fc2_all.reshape(units // wide, width).astype(F32)
    grad_qkv, grad_out, grad_router, grad_mix, grad_gain_one, grad_gain_two = put_heads(
        ids, gather_pieces(heads_sum), w_qkv, gain_one, experts
    )
    return (
        output[None],
        input_grad[None],
        grad_qkv,
        grad_out,
        grad_fc1,
        grad_fc2,
        grad_router.T,
        grad_mix.T,
        grad_gain_one.reshape(held),
        grad_gain_two.reshape(held),
        grad_expert_in[None],
        grad_expert_out[None],
    )


def solution(mesh):
    return jax.shard_map(
        per_device,
        mesh=mesh,
        in_specs=(
            P("wide", "narrow", None),
            P("wide", None),
            P(("narrow", "wide"), None),
            P(),
            P(),
            P(),
            P(),
            P(),
            P(),
            P(),
            P(),
            P("wide", None, None),
            P("wide", None, None),
            P("wide", "narrow", None),
        ),
        out_specs=(
            P("wide", "narrow", None),
            P("wide", "narrow", None),
            P("wide", None),
            P("wide", None),
            P("wide", None),
            P("wide", None),
            P("wide", None),
            P("wide", None),
            P("wide"),
            P("wide"),
            P("wide", "narrow", None),
            P("wide", "narrow", None),
        ),
        check_vma=False,
    )
```
